256 devices in a mesh: dp: 64 (over z, x, core), tp: 4 (over y).
Axes of the slice: x: 4, y: 4, z: 8, core: 2. Of those that a mesh axis runs over, the one named last changes fastest.
Arguments:
- pool: bfloat16 [3584, 128, 576], P('dp'), may hold values from -6 to 6
- pool_owner: int32 [3584], P('dp'), may hold values from 0 to 63, as said below
- pool_slot: int32 [3584], P('dp'), may hold values from 0 to 127, as said below
- req_len: int32 [128], P('dp'), may hold values from 1 to 16256, as said below
- query: bfloat16 [2, 128, 80, 576], P(None, 'dp', 'tp'), may hold values from -16 to 16
- new_kv: bfloat16 [2, 128, 576], P(None, 'dp')
- resid: bfloat16 [2, 128, 7168], P(None, None, 'dp'), may hold values from -6 to 6
- w_uv: bfloat16 [80, 512, 128], P('tp'), may hold values from -1 to 1
- w_out: bfloat16 [10240, 7168], P('tp', 'dp'), may hold values from -0.0625 to 0.0625
- ffn_gain: float32 [7168], replicated, may hold values from 0.25 to 1.75
- w_gate: bfloat16 [7168, 9216], P(None, ('dp', 'tp')), may hold values from -0.0625 to 0.0625
- w_up: bfloat16 [7168, 9216], P(None, ('dp', 'tp')), may hold values from -0.0625 to 0.0625
- w_down: bfloat16 [9216, 7168], P(('dp', 'tp')), may hold values from -0.25 to 0.25
Outputs:
- attended: bfloat16 [2, 128, 7168], P(None, None, 'dp')
- layer_out: bfloat16 [2, 128, 7168], P(None, None, ('dp', 'tp'))
The draws below stay inside these ranges and needn't reach their ends.
Inputs may be any that keep to these rules, and one draw needn't show every extreme that they name: `pool_owner`: each device hands at most 2 of its blocks to one owner group; one group receives exactly 2 blocks from every device; every group receives at least 2 blocks. `pool_slot`: the blocks that one group receives take the positions 0 up to their number less one, each once. The two requests of a group hold exactly the blocks that the group receives: ceil(req_len / 128) blocks each.
All inputs are finite; a program needn't handle non-finite values.
Results may differ from the reference program's by a relative error of at most 0.025.
Values may be sent and summed in bfloat16 or wider, within the bound.
A program may use at most 192 MiB of HBM per device.

```python
import jax
import jax.numpy as jnp
from jax import lax

D = 7168
H = 80
LAT = 512
ROPE = 64
KV = 576
VD = 128
FF = 9216
BLK = 128
REQ = 2
STEPS = 2
NB_DEV = 56
NBT = 3584
REQ_ALL = 128
CAPB = 128


def permute_one(subkey):
    return jax.random.permutation(subkey, NB_DEV).astype(jnp.int32)


def handoff_lists(key):
    groups = REQ_ALL // REQ
    others = groups - 1
    subkeys = jax.random.split(key, 7)
    heavy_owner = jax.random.randint(subkeys[0], (), 0, groups, dtype=jnp.int32)
    rest_ids = jnp.arange(others, dtype=jnp.int32)
    rest_ids = rest_ids + (rest_ids >= heavy_owner).astype(jnp.int32)
    senders = jnp.arange(groups, dtype=jnp.int32)
    first_pick = senders % others
    second_pick = (senders + 1) % others
    forced = jnp.zeros((groups, others), jnp.int32)
    forced = forced.at[senders, first_pick].add(1).at[senders, second_pick].add(1)
    owner_bias = jax.random.randint(subkeys[1], (others,), 0, groups, dtype=jnp.int32)
    jitter_values = jax.random.randint(subkeys[2], (groups, others, 2), 0, groups, dtype=jnp.int32)
    unit_index = jnp.arange(others * 2, dtype=jnp.int32).reshape(others, 2)
    unit_score = (jitter_values + owner_bias[None, :, None]) * (4 * groups) + unit_index[None]
    usable = jnp.arange(2, dtype=jnp.int32)[None, None, :] >= forced[:, :, None]
    unit_score = jnp.where(usable, unit_score, -1).reshape(groups, others * 2)
    chosen_values, chosen = lax.top_k(unit_score, NB_DEV - 4)
    picked = rest_ids[chosen // 2]
    heavy_cols = jnp.full((groups, 2), heavy_owner, jnp.int32)
    destinations = jnp.concatenate([heavy_cols, rest_ids[first_pick][:, None], rest_ids[second_pick][:, None], picked], axis=1)
    shuffle = jax.vmap(permute_one)(jax.random.split(subkeys[3], groups))
    destinations = jnp.take_along_axis(destinations, shuffle, axis=1)
    owner_ids = destinations.reshape(groups * NB_DEV).astype(jnp.int32)
    priority = jax.random.permutation(subkeys[4], groups * NB_DEV).astype(jnp.int32)
    same_owner = owner_ids[:, None] == owner_ids[None, :]
    slot_ids = jnp.sum(same_owner & (priority[None, :] < priority[:, None]), axis=1).astype(jnp.int32)
    owner_load = jnp.sum((owner_ids[:, None] == jnp.arange(groups, dtype=jnp.int32)[None, :]).astype(jnp.int32), axis=0)
    first_count = jax.random.randint(subkeys[5], (groups,), 1, owner_load, dtype=jnp.int32)
    first_count = jnp.where(jnp.arange(groups, dtype=jnp.int32) == heavy_owner, owner_load - 1, first_count)
    counts = jnp.stack([first_count, owner_load - first_count], axis=1)
    row_tail = jax.random.randint(subkeys[6], (groups, 2), 1, BLK + 1, dtype=jnp.int32)
    row_tail = row_tail.at[heavy_owner, 0].set(BLK)
    lengths = ((counts - 1) * BLK + row_tail).reshape(groups * REQ).astype(jnp.int32)
    return (owner_ids, slot_ids, lengths)


def latent_rows(key):
    return jax.random.normal(jax.random.fold_in(key, 41), (STEPS, REQ_ALL, KV), jnp.float32)


def draw_pool_owner(key, part):
    shared = handoff_lists(key)
    return shared[0]


def draw_pool_slot(key, part):
    shared = handoff_lists(key)
    return shared[1]


def draw_req_len(key, part):
    shared = handoff_lists(key)
    return shared[2]


def draw_new_kv(key, part):
    return latent_rows(key).astype(jnp.bfloat16)


def draw_query(key, part):
    key = jax.random.fold_in(key, 7)
    subkeys = jax.random.split(key, 1)
    values = jax.random.normal(subkeys[0], (STEPS, REQ_ALL, H, KV), jnp.float32)
    return jnp.clip(values, -16.0, 16.0).astype(jnp.bfloat16)


def spiked(entries, own_key, source, target, shards_of, factor):
    def block_of(axis_at):
        return (jnp.arange(entries.shape[axis_at]) // (entries.shape[axis_at] // shards_of)).reshape((-1,) + (1,) * (entries.ndim - 1 - axis_at))

    first = jax.random.permutation(own_key, shards_of)[block_of(target)]
    second = (block_of(target) + shards_of // 2) % shards_of
    return jnp.where((block_of(source) == first) | (block_of(source) == second), factor * entries, entries)


def block_levels(rng, dims, pieces, low, largest):
    def one(dim, blocks):
        steps = jax.random.uniform(jax.random.fold_in(jax.random.fold_in(rng, 6), dim), (blocks,), jnp.float32, low / len(pieces), largest / len(pieces))
        return jnp.repeat(jnp.exp(steps), dims[dim] // blocks).reshape((-1,) + (1,) * (len(dims) - dim - 1))

    factor_of = one(*pieces[0])
    for cut in pieces[1:]:
        factor_of = factor_of * one(*cut)
    return factor_of


def scatter_about(key, shape, scale, most, pieces=(), kind=jnp.bfloat16):
    array = jax.random.normal(key, shape, jnp.float32) * scale
    if len(pieces) > 0:
        array = block_levels(key, shape, pieces, -0.22, 0.18) * array
    return jnp.clip(array, min=-most, max=most).astype(kind)


def gaussian_with(stream_key, dims, scale, limit, cuts, heavy, held_as=jnp.bfloat16):
    drawn = scale * jax.random.normal(stream_key, dims, jnp.float32)
    if cuts:
        drawn = drawn * block_levels(stream_key, dims, cuts, -0.22, 0.18)
    return jnp.clip(spiked(drawn, jax.random.fold_in(stream_key, 3), *heavy), -limit, limit).astype(held_as)


def setup_inputs(seed: int = 0) -> dict:
    streams_of = jax.random.split(jax.random.key(seed), 14)
    pool = scatter_about(streams_of[0], (NBT, BLK, KV), 1.0, 6.0, ((0, 64),))
    pool_owner = draw_pool_owner(jax.random.fold_in(streams_of[13], 71), 0)
    pool_slot = draw_pool_slot(jax.random.fold_in(streams_of[13], 71), 0)
    req_len = draw_req_len(jax.random.fold_in(streams_of[13], 71), 0)
    query = draw_query(jax.random.fold_in(streams_of[13], 71), 0)
    new_kv = draw_new_kv(jax.random.fold_in(streams_of[13], 71), 0)
    resid = scatter_about(streams_of[6], (STEPS, REQ_ALL, D), 0.5, 6.0, ((2, 64),))
    w_uv = scatter_about(streams_of[7], (H, LAT, VD), 32 ** -0.5, 1.0, ((0, 4),))
    w_out = scatter_about(streams_of[8], (H * VD, D), (H * VD) ** -0.5, 0.0625, ((0, 4), (1, 64)))
    ffn_gain = jnp.clip(1.0 + 0.15 * jax.random.normal(streams_of[9], (D,), jnp.float32), 0.25, 1.75)
    w_gate = scatter_about(streams_of[10], (D, FF), D ** -0.5, 0.0625, ((1, 256),))
    w_up = scatter_about(streams_of[11], (D, FF), D ** -0.5, 0.0625, ((1, 256),))
    w_down = gaussian_with(streams_of[12], (FF, D), FF ** -0.5, 0.25, ((0, 256),), (0, 1, 256, 6.0))
    return dict(pool=pool, pool_owner=pool_owner, pool_slot=pool_slot, req_len=req_len, query=query, new_kv=new_kv, resid=resid, w_uv=w_uv, w_out=w_out, ffn_gain=ffn_gain, w_gate=w_gate, w_up=w_up, w_down=w_down)


epsilon = 1e-06

def reference(pool, pool_owner, pool_slot, req_len, query, new_kv, resid, w_uv, w_out, ffn_gain, w_gate, w_up, w_down):
    groups = REQ_ALL // REQ
    score_scale = (3 * ROPE) ** (-0.5)
    block_index = jnp.arange(NBT, dtype=jnp.int32)
    position = (pool_owner * CAPB + pool_slot).astype(jnp.int32)
    source_map = jnp.full((groups * CAPB,), -1, jnp.int32).at[position].set(block_index).reshape(groups, CAPB)
    lengths = req_len.reshape(groups, REQ)
    queries = jnp.transpose(query.reshape(STEPS, groups, REQ, H, KV), (1, 0, 2, 3, 4))
    new_rows = jnp.transpose(new_kv.reshape(STEPS, groups, REQ, KV), (1, 0, 2, 3))
    visible = jnp.arange(STEPS)[None, :] <= jnp.arange(STEPS)[:, None]

    def one_group(inputs):
        sources, group_len, group_query, group_new = inputs
        cached = pool[jnp.maximum(sources, 0)]
        first_blocks = (group_len[0] + BLK - 1) // BLK
        positions = jnp.arange(CAPB, dtype=jnp.int32)
        second = positions >= first_blocks
        within = positions - jnp.where(second, first_blocks, 0)
        row_index = within[:, None] * BLK + jnp.arange(BLK, dtype=jnp.int32)[None, :]
        row_limit = jnp.where(second, group_len[1], group_len[0])
        usable = (sources >= 0)[:, None] & (row_index < row_limit[:, None])
        owner_mask = jnp.stack([usable & ~second[:, None], usable & second[:, None]])
        query_f32 = group_query.astype(jnp.float32)
        cache_scores = jnp.einsum('trhk,sbk->trhsb', query_f32, cached.astype(jnp.float32)) * score_scale
        new_scores = jnp.einsum('trhk,urk->trhu', query_f32, group_new.astype(jnp.float32)) * score_scale
        cache_mask = owner_mask[None, :, None, :, :]
        new_mask = visible[:, None, None, :]
        peak_cache = lax.optimization_barrier(jnp.max(jnp.where(cache_mask, cache_scores, -jnp.inf), axis=(3, 4)))
        peak_new = lax.optimization_barrier(jnp.max(jnp.where(new_mask, new_scores, -jnp.inf), axis=3))
        overall = jnp.maximum(peak_cache, peak_new)
        cache_weights = jnp.where(cache_mask, jnp.exp(cache_scores - overall[..., None, None]), 0.0)
        new_weights = jnp.where(new_mask, jnp.exp(new_scores - overall[..., None]), 0.0)
        weight_sum = lax.optimization_barrier(jnp.sum(cache_weights, axis=(3, 4))) + lax.optimization_barrier(jnp.sum(new_weights, axis=3))
        cache_rounded = lax.optimization_barrier(cache_weights.astype(jnp.bfloat16)).astype(jnp.float32)
        new_rounded = lax.optimization_barrier(new_weights.astype(jnp.bfloat16)).astype(jnp.float32)
        weighted = jnp.einsum('trhsb,sbl->trhl', cache_rounded, cached[..., :LAT].astype(jnp.float32))
        weighted = weighted + jnp.einsum('trhu,url->trhl', new_rounded, group_new[..., :LAT].astype(jnp.float32))
        latent_out = lax.optimization_barrier((weighted / weight_sum[..., None]).astype(jnp.bfloat16)).astype(jnp.float32)
        head_out = jnp.einsum('trhl,hlv->trhv', latent_out, w_uv.astype(jnp.float32))
        return head_out.astype(jnp.bfloat16).reshape(STEPS, REQ, H * VD)
    head_out = lax.map(one_group, (source_map, lengths, queries, new_rows))
    head_out = jnp.transpose(head_out, (1, 0, 2, 3)).reshape(STEPS * REQ_ALL, H * VD)
    projected = jnp.dot(head_out, w_out, preferred_element_type=jnp.float32)
    residual_sum = resid.reshape(STEPS * REQ_ALL, D).astype(jnp.float32) + projected
    attended = residual_sum.astype(jnp.bfloat16)
    attended_f32 = lax.optimization_barrier(attended).astype(jnp.float32)
    mean_square = lax.optimization_barrier(jnp.mean(attended_f32 * attended_f32, axis=1, keepdims=True))
    normed = (attended_f32 * lax.rsqrt(mean_square + epsilon) * ffn_gain).astype(jnp.bfloat16)
    gate_values = jnp.dot(normed, w_gate, preferred_element_type=jnp.float32)
    up_values = jnp.dot(normed, w_up, preferred_element_type=jnp.float32)
    hidden = (jax.nn.silu(gate_values) * up_values).astype(jnp.bfloat16)
    down_values = jnp.dot(hidden, w_down, preferred_element_type=jnp.float32)
    layer_out = (attended_f32 + down_values).astype(jnp.bfloat16)
    return (attended.reshape(STEPS, REQ_ALL, D), layer_out.reshape(STEPS, REQ_ALL, D))
```

```python
import functools
import jax
import jax.numpy as jnp
from jax import lax
from jax.experimental import pallas as pl
from jax.experimental.pallas import tpu as pltpu
from jax.sharding import PartitionSpec as P

NZ, NX, NC = 8, 4, 2
NDP = NZ * NX * NC
LOW = -3.0e38
BIG = 56 * 1024 * 1024


def place():
    d = lax.axis_index("dp")
    return lax.div(d, 8), lax.rem(lax.div(d, 2), 4), lax.rem(d, 2), lax.axis_index("tp")


def dp_of(z, x, c):
    return (z * NX + x) * NC + c


def greet(peers):
    barrier = pltpu.get_barrier_semaphore()
    for peer in peers:
        pl.semaphore_signal(barrier, inc=1, device_id=peer, device_id_type=pl.DeviceIdType.MESH)
    pl.semaphore_wait(barrier, len(peers))


def gather_kernel(x_ref, out_ref, send, recv, own_sem):
    z, x, c, tp = place()
    up, down = lax.rem(z + 1, NZ), lax.rem(z + NZ - 1, NZ)
    right, left = lax.rem(x + 1, NX), lax.rem(x + NX - 1, NX)
    to_up, to_down = (dp_of(up, x, c), tp), (dp_of(down, x, c), tp)
    to_right, to_left = (dp_of(z, right, c), tp), (dp_of(z, left, c), tp)
    to_twin = (dp_of(z, x, 1 - c), tp)
    greet((to_up, to_down, to_right, to_left, to_twin))
    me = dp_of(z, x, c)
    started = []

    def push(chunk, peer, own=False):
        copy = pltpu.make_async_remote_copy(
            src_ref=x_ref if own else out_ref.at[chunk],
            dst_ref=out_ref.at[chunk],
            send_sem=send.at[len(started)],
            recv_sem=recv.at[chunk],
            device_id=peer,
            device_id_type=pl.DeviceIdType.MESH,
        )
        copy.start()
        started.append(copy)

    def arrived(chunk):
        pltpu.make_async_remote_copy(
            src_ref=x_ref,
            dst_ref=out_ref.at[chunk],
            send_sem=send.at[0],
            recv_sem=recv.at[chunk],
            device_id=to_twin,
            device_id_type=pl.DeviceIdType.MESH,
        ).wait_recv()

    own_copy = pltpu.make_async_copy(x_ref, out_ref.at[me], own_sem)
    own_copy.start()

    def along_z(step, sign, own=False):
        at = lax.rem(z + NZ - sign * step, NZ)
        chunk = dp_of(at, x, c)
        if not own:
            arrived(chunk)
        if own:
            push(chunk, to_up, own)
            push(chunk, to_down, own)
        elif sign > 0 and step < 4:
            push(chunk, to_up)
        elif sign < 0 and step < 3:
            push(chunk, to_down)
        push(chunk, to_right, own)
        push(chunk, to_left, own)
        push(chunk, to_twin, own)

    def along_x(step, sign):
        at = lax.rem(z + NZ - sign * step, NZ)
        even = step % 2 == 0
        first, second = dp_of(at, left, c), dp_of(at, right, c)
        arrived(first)
        if even:
            push(first, to_right)
        push(first, to_twin)
        arrived(second)
        if not even:
            push(second, to_left)
        push(second, to_twin)

    def across(step, sign):
        at = lax.rem(z + NZ - sign * step, NZ)
        far = dp_of(at, lax.rem(x + 2, NX), c)
        arrived(far)
        push(far, to_twin)

    order = [(0, 1), (1, 1), (1, -1), (2, 1), (2, -1), (3, 1), (3, -1), (4, 1)]
    along_z(0, 1, own=True)
    along_z(1, 1)
    along_z(1, -1)
    for index, (step, sign) in enumerate(order):
        along_x(step, sign)
        if index + 3 < len(order):
            along_z(*order[index + 3])
        if index >= 1:
            across(*order[index - 1])
    across(*order[-1])
    for at_z in range(NZ):
        for at_x in range(NX):
            arrived(dp_of(at_z, at_x, 1 - c))
    own_copy.wait()
    for copy in started:
        copy.wait_send()


def gather_dp(shard, collective_id, space=None):
    space = pl.ANY if space is None else space
    return pl.pallas_call(
        gather_kernel,
        out_shape=jax.ShapeDtypeStruct((NDP,) + shard.shape, shard.dtype),
        in_specs=[pl.BlockSpec(memory_space=space)],
        out_specs=pl.BlockSpec(memory_space=space),
        scratch_shapes=[
            pltpu.SemaphoreType.DMA((63,)),
            pltpu.SemaphoreType.DMA((NDP,)),
            pltpu.SemaphoreType.DMA,
        ],
        compiler_params=pltpu.CompilerParams(
            collective_id=collective_id, has_side_effects=True, vmem_limit_bytes=BIG
        ),
        name="gather_dp",
    )(shard)


def flat_gather_kernel(x_ref, out_ref, send, recv, own_sem):
    z, x, c, tp = place()
    z_peers = [lax.rem(z + k, NZ) for k in (1, 7, 2, 6, 3, 5, 4)]
    x_peers = [lax.rem(x + k, NX) for k in (1, 3, 2)]
    twin = (dp_of(z, x, 1 - c), tp)
    greet([(dp_of(k, x, c), tp) for k in z_peers] + [(dp_of(z, k, c), tp) for k in x_peers] + [twin])
    own = pltpu.make_async_copy(x_ref, out_ref.at[z, x, c], own_sem)
    own.start()

    def remote(src, dst, number, peer):
        return pltpu.make_async_remote_copy(
            src_ref=src,
            dst_ref=dst,
            send_sem=send.at[number],
            recv_sem=recv.at[number],
            device_id=peer,
            device_id_type=pl.DeviceIdType.MESH,
        )

    first = [
        remote(x_ref, out_ref.at[z, x, c], k, (dp_of(peer, x, c), tp))
        for k, peer in enumerate(z_peers)
    ]
    for copy in first:
        copy.start()
    own.wait()
    for copy in first:
        copy.wait_recv()
    second = [
        remote(out_ref.at[:, x, c], out_ref.at[:, x, c], 7 + k, (dp_of(z, peer, c), tp))
        for k, peer in enumerate(x_peers)
    ]
    for copy in second:
        copy.start()
    third = [remote(out_ref.at[:, x, c], out_ref.at[:, x, c], 10, twin)]
    third[0].start()
    for k, copy in enumerate(second):
        copy.wait_recv()
        at = lax.rem(x + (3, 1, 2)[k], NX)
        third.append(remote(out_ref.at[:, at, c], out_ref.at[:, at, c], 11 + k, twin))
        third[-1].start()
    for copy in third:
        copy.wait_recv()
    for copy in first + second + third:
        copy.wait_send()


def flat_gather_dp(shard, collective_id):
    vmem = pl.BlockSpec(memory_space=pltpu.VMEM)
    return pl.pallas_call(
        flat_gather_kernel,
        out_shape=jax.ShapeDtypeStruct((NZ, NX, NC) + shard.shape, shard.dtype),
        in_specs=[vmem],
        out_specs=vmem,
        scratch_shapes=[
            pltpu.SemaphoreType.DMA((14,)),
            pltpu.SemaphoreType.DMA((14,)),
            pltpu.SemaphoreType.DMA,
        ],
        compiler_params=pltpu.CompilerParams(
            collective_id=collective_id, has_side_effects=True, vmem_limit_bytes=BIG
        ),
        name="flat_gather_dp",
    )(shard)


def attend_kernel(owner_ref, slot_ref, part_ref, lim0_ref, lim1_ref, q_ref, blk_ref, new_ref, wuv_ref,
                  out_ref, stat_ref, acc, top, tot, table, *, per_step, blocks, heads):
    step = pl.program_id(0)
    rows = 2 * heads
    lat = wuv_ref.shape[1]
    scale = (3 * 64) ** (-0.5)
    width = blk_ref.shape[2]

    @pl.when(step == 0)
    def _():
        def clear(i, _):
            at = pl.multiple_of(i * 128, 128)
            for k in range(lat // 128):
                acc[k, pl.ds(at, 128), :] = jnp.zeros((128, 128), jnp.float32)
            top[pl.ds(at, 128), :] = jnp.full((128, 128), LOW, jnp.float32)
            tot[pl.ds(at, 128), :] = jnp.zeros((128, 128), jnp.float32)
            return 0

        lax.fori_loop(0, acc.shape[1] // 128, clear, 0)

    lane = lax.broadcasted_iota(jnp.int32, (rows, width), 1)
    late = lax.broadcasted_iota(jnp.int32, (rows, width), 0) >= heads

    def one(number, block):
        group, slot, part = owner_ref[number], slot_ref[number], part_ref[number]
        limit = jnp.where(late, lim1_ref[number], lim0_ref[number])
        both = jnp.dot(q_ref[group, :, :block.shape[0]], block, preferred_element_type=jnp.float32)
        scores = jnp.where(part == 0, both[:rows], both[rows:]) * scale
        keep = lane < limit
        peak = jnp.max(jnp.where(keep, scores, LOW), axis=1, keepdims=True)
        at = pl.multiple_of((slot * 2 + part) * rows, 8)
        old = top[pl.ds(at, rows), :]
        now = jnp.maximum(old, peak)
        weights = jnp.where(keep, jnp.exp(scores - now[:, :1]), 0.0)
        fade = jnp.exp(old - now)
        top[pl.ds(at, rows), :] = now
        tot[pl.ds(at, rows), :] = tot[pl.ds(at, rows), :] * fade + jnp.sum(weights, axis=1, keepdims=True)
        mixed = lax.dot_general(
            weights.astype(jnp.bfloat16), block[:lat], (((1,), (1,)), ((), ())),
            preferred_element_type=jnp.float32,
        )
        for k in range(lat // 128):
            acc[k, pl.ds(at, rows), :] = (
                acc[k, pl.ds(at, rows), :] * fade + mixed[:, k * 128:(k + 1) * 128])

    for k in range(per_step):
        one(step * per_step + k, blk_ref[k])

    @pl.when(step == pl.num_programs(0) - 1)
    def _():
        one(blocks, new_ref[0])
        one(blocks + 1, new_ref[1])

        def head(h, _):
            every = pl.ds(h, acc.shape[1] // heads, stride=heads)
            latent = jnp.concatenate([acc[k, every, :] for k in range(lat // 128)], axis=1).astype(jnp.bfloat16)
            table[every, :] = jnp.dot(
                latent, wuv_ref[h], preferred_element_type=jnp.float32)
            return 0

        lax.fori_loop(0, heads, head, 0)
        out_ref[...] = table[...].astype(jnp.bfloat16).reshape(out_ref.shape)
        column = lax.broadcasted_iota(jnp.int32, (2 * rows, 128), 1)

        def gather(j, carry):
            at = pl.multiple_of(j * 2 * rows, 8)
            return (jnp.where(column == j, top[pl.ds(at, 2 * rows), :], carry[0]),
                    jnp.where(column == j, tot[pl.ds(at, 2 * rows), :], carry[1]))

        zero = jnp.zeros((2 * rows, 128), jnp.float32)
        tops, tots = lax.fori_loop(0, NDP, gather, (zero, zero))
        pad = jnp.zeros((128 - 2 * rows, 128), jnp.float32)
        stat_ref[0] = jnp.concatenate([tops, pad], axis=0).T[:NDP]
        stat_ref[1] = jnp.concatenate([tots, pad], axis=0).T[:NDP]


def attend(owner, slot, part, lim0, lim1, q_all, pool_t, new_t, w_uv, per_step=8):
    blocks, key, width = pool_t.shape
    heads, lat, vd = w_uv.shape
    total = NDP * 4 * heads
    vmem = pl.BlockSpec(memory_space=pltpu.VMEM)
    return pl.pallas_call(
        functools.partial(attend_kernel, per_step=per_step, blocks=blocks, heads=heads),
        out_shape=(
            jax.ShapeDtypeStruct((NDP, 4 * heads, vd), jnp.bfloat16),
            jax.ShapeDtypeStruct((2, NDP, 128), jnp.float32),
        ),
        grid_spec=pltpu.PrefetchScalarGridSpec(
            num_scalar_prefetch=5,
            grid=(blocks // per_step,),
            in_specs=[
                vmem,
                pl.BlockSpec((per_step, key, width), lambda i, *_: (i, 0, 0)),
                vmem,
                vmem,
            ],
            out_specs=[vmem, vmem],
            scratch_shapes=[
                pltpu.VMEM((lat // 128, total, 128), jnp.float32),
                pltpu.VMEM((total, 128), jnp.float32),
                pltpu.VMEM((total, 128), jnp.float32),
                pltpu.VMEM((total, vd), jnp.float32),
            ],
        ),
        compiler_params=pltpu.CompilerParams(vmem_limit_bytes=BIG, dimension_semantics=("arbitrary",)),
        name="attend",
    )(owner, slot, part, lim0, lim1, q_all, pool_t, new_t, w_uv)


def fold_softmax_kernel(h_ref, st_ref, out_ref, c_buf, c_st, mine, m_st, x_buf, x_st, z_src, z_st, z_buf, z_in,
                        send, recv):
    z, x, c, tp = place()
    z_peers = [lax.rem(z + k, NZ) for k in (1, 7, 2, 6, 3, 5, 4)]
    x_peers = [lax.rem(x + k, NX) for k in (1, 3, 2)]
    twin = (dp_of(z, x, 1 - c), tp)
    greet([(dp_of(k, x, c), tp) for k in z_peers] + [(dp_of(z, k, c), tp) for k in x_peers] + [twin])

    def remote(src, dst, number, peer):
        copy = pltpu.make_async_remote_copy(
            src_ref=src, dst_ref=dst, send_sem=send.at[number], recv_sem=recv.at[number],
            device_id=peer, device_id_type=pl.DeviceIdType.MESH,
        )
        copy.start()
        return copy

    half = NDP // 2
    there = pl.multiple_of((1 - c) * half, half)
    here = pl.multiple_of(c * half, half)
    one = remote(h_ref.at[pl.ds(there, half)], c_buf, 0, twin)
    two = remote(st_ref.at[:, pl.ds(there, half)], c_st, 1, twin)
    one.wait()
    two.wait()

    def merge(stats):
        tops = stats[0][0]
        for s in stats[1:]:
            tops = jnp.maximum(tops, s[0])
        factors = [jnp.exp(s[0] - tops) for s in stats]
        total = sum(f * s[1] for f, s in zip(factors, stats))
        pad = 128 - tops.shape[0]
        columns = [
            jnp.concatenate([f, jnp.zeros((pad, 128), jnp.float32)], axis=0).T if pad else f.T
            for f in factors
        ]
        return tops, total, columns

    rows = h_ref.shape[1]
    tops, total, columns = merge([st_ref[:, pl.ds(here, half), :], c_st[...]])
    m_st[0] = tops
    m_st[1] = total
    for j in range(half):
        mine[j] = (
            h_ref[here + j].astype(jnp.float32) * columns[0][:rows, j:j + 1]
            + c_buf[j].astype(jnp.float32) * columns[1][:rows, j:j + 1]
        ).astype(jnp.bfloat16)
    copies = []
    for k, peer in enumerate(x_peers):
        at = pl.multiple_of(peer * NZ, NZ)
        dst = (dp_of(z, peer, c), tp)
        copies.append(remote(mine.at[pl.ds(at, NZ)], x_buf.at[k], 2 + 2 * k, dst))
        copies.append(remote(m_st.at[:, pl.ds(at, NZ)], x_st.at[k], 3 + 2 * k, dst))
    for copy in copies:
        copy.wait()
    at = pl.multiple_of(x * NZ, NZ)
    tops, total, columns = merge([m_st[:, pl.ds(at, NZ), :]] + [x_st[k] for k in range(3)])
    for j in range(NZ):
        z_src[j] = (
            mine[at + j].astype(jnp.float32) * columns[0][:rows, j:j + 1]
            + sum(x_buf[k, j].astype(jnp.float32) * columns[k + 1][:rows, j:j + 1] for k in range(3))
        ).astype(jnp.bfloat16)
        z_st[j, 0:1, :] = tops[j:j + 1]
        z_st[j, 1:2, :] = total[j:j + 1]
        z_st[j, 2:8, :] = jnp.zeros((6, 128), jnp.float32)
    copies = []
    for k, peer in enumerate(z_peers):
        dst = (dp_of(peer, x, c), tp)
        copies.append(remote(z_src.at[peer], z_buf.at[k], 8 + 2 * k, dst))
        copies.append(remote(z_st.at[peer], z_in.at[k], 9 + 2 * k, dst))
    for copy in copies:
        copy.wait()
    stats = [z_st[z]] + [z_in[k] for k in range(7)]
    tops = jnp.concatenate([s[0:1] for s in stats], axis=0)
    tots = jnp.concatenate([s[1:2] for s in stats], axis=0)
    peak = jnp.max(tops, axis=0, keepdims=True)
    factor = jnp.exp(tops - peak)
    share = factor / jnp.sum(factor * tots, axis=0, keepdims=True)
    columns = jnp.concatenate([share, jnp.zeros((120, 128), jnp.float32)], axis=0).T
    final = z_src[z].astype(jnp.float32) * columns[:rows, 0:1]
    for k in range(7):
        final = final + z_buf[k].astype(jnp.float32) * columns[:rows, k + 1:k + 2]
    out_ref[...] = final.astype(jnp.bfloat16)


def fold_softmax(h, st, collective_id):
    vmem = pl.BlockSpec(memory_space=pltpu.VMEM)
    _, rows, vd = h.shape
    bf, f32 = jnp.bfloat16, jnp.float32
    return pl.pallas_call(
        fold_softmax_kernel,
        out_shape=jax.ShapeDtypeStruct((rows, vd), bf),
        in_specs=[vmem, vmem],
        out_specs=vmem,
        scratch_shapes=[
            pltpu.VMEM((32, rows, vd), bf), pltpu.VMEM((2, 32, 128), f32),
            pltpu.VMEM((32, rows, vd), bf), pltpu.VMEM((2, 32, 128), f32),
            pltpu.VMEM((3, NZ, rows, vd), bf), pltpu.VMEM((3, 2, NZ, 128), f32),
            pltpu.VMEM((NZ, rows, vd), bf), pltpu.VMEM((NZ, 8, 128), f32),
            pltpu.VMEM((7, rows, vd), bf), pltpu.VMEM((7, 8, 128), f32),
            pltpu.SemaphoreType.DMA((22,)), pltpu.SemaphoreType.DMA((22,)),
        ],
        compiler_params=pltpu.CompilerParams(
            collective_id=collective_id, has_side_effects=True, vmem_limit_bytes=BIG),
        name="fold_softmax",
    )(h, st)


def fold_sum_kernel(h_ref, out_ref, c_buf, mine, x_buf, z_src, z_buf, send, recv):
    z, x, c, tp = place()
    z_peers = [lax.rem(z + k, NZ) for k in (1, 7, 2, 6, 3, 5, 4)]
    x_peers = [lax.rem(x + k, NX) for k in (1, 3, 2)]
    twin = (dp_of(z, x, 1 - c), tp)
    greet([(dp_of(k, x, c), tp) for k in z_peers] + [(dp_of(z, k, c), tp) for k in x_peers] + [twin])

    def remote(src, dst, number, peer):
        copy = pltpu.make_async_remote_copy(
            src_ref=src, dst_ref=dst, send_sem=send.at[number], recv_sem=recv.at[number],
            device_id=peer, device_id_type=pl.DeviceIdType.MESH,
        )
        copy.start()
        return copy

    f32, bf = jnp.float32, jnp.bfloat16
    remote(h_ref.at[:, :, 1 - c], c_buf, 0, twin).wait()
    for k in range(NX):
        mine[:, k] = (h_ref[:, k, c].astype(f32) + c_buf[:, k].astype(f32)).astype(bf)
    copies = [
        remote(mine.at[:, peer], x_buf.at[k], 1 + k, (dp_of(z, peer, c), tp))
        for k, peer in enumerate(x_peers)
    ]
    for copy in copies:
        copy.wait()
    for j in range(NZ):
        z_src[j] = (mine[j, x].astype(f32) + sum(x_buf[k, j].astype(f32) for k in range(3))).astype(bf)
    copies = [
        remote(z_src.at[peer], z_buf.at[k], 4 + k, (dp_of(peer, x, c), tp))
        for k, peer in enumerate(z_peers)
    ]
    for copy in copies:
        copy.wait()
    out_ref[...] = z_src[z].astype(f32) + sum(z_buf[k].astype(f32) for k in range(7))


def fold_sum(h, collective_id):
    vmem = pl.BlockSpec(memory_space=pltpu.VMEM)
    rows, width = h.shape[3:]
    bf = jnp.bfloat16
    return pl.pallas_call(
        fold_sum_kernel,
        out_shape=jax.ShapeDtypeStruct((rows, width), jnp.float32),
        in_specs=[vmem],
        out_specs=vmem,
        scratch_shapes=[
            pltpu.VMEM((NZ, NX, rows, width), bf),
            pltpu.VMEM((NZ, NX, rows, width), bf),
            pltpu.VMEM((3, NZ, rows, width), bf),
            pltpu.VMEM((NZ, rows, width), bf),
            pltpu.VMEM((7, rows, width), bf),
            pltpu.SemaphoreType.DMA((11,)), pltpu.SemaphoreType.DMA((11,)),
        ],
        compiler_params=pltpu.CompilerParams(
            collective_id=collective_id, has_side_effects=True, vmem_limit_bytes=BIG),
        name="fold_sum",
    )(h)


def swap_tp_kernel(x_ref, out_ref, send, recv, own_sem, *, spread):
    d = lax.axis_index("dp")
    tp = lax.axis_index("tp")
    peers = [lax.rem(tp + k, 4) for k in (1, 3, 2)]
    greet([(d, k) for k in peers])
    copies = []
    for k, peer in enumerate(peers):
        copy = pltpu.make_async_remote_copy(
            src_ref=x_ref if spread else x_ref.at[peer], dst_ref=out_ref.at[tp],
            send_sem=send.at[k], recv_sem=recv.at[k],
            device_id=(d, peer), device_id_type=pl.DeviceIdType.MESH,
        )
        copy.start()
        copies.append(copy)
    own = pltpu.make_async_copy(x_ref if spread else x_ref.at[tp], out_ref.at[tp], own_sem)
    own.start()
    own.wait()
    for copy in copies:
        copy.wait()


def swap_tp(v, collective_id, spread):
    vmem = pl.BlockSpec(memory_space=pltpu.VMEM)
    return pl.pallas_call(
        functools.partial(swap_tp_kernel, spread=spread),
        out_shape=jax.ShapeDtypeStruct(((4,) + v.shape) if spread else v.shape, v.dtype),
        in_specs=[vmem],
        out_specs=vmem,
        scratch_shapes=[
            pltpu.SemaphoreType.DMA((3,)), pltpu.SemaphoreType.DMA((3,)), pltpu.SemaphoreType.DMA,
        ],
        compiler_params=pltpu.CompilerParams(
            collective_id=collective_id, has_side_effects=True, vmem_limit_bytes=BIG),
        name="swap_tp",
    )(v)


epsilon = 1e-06


def per_device(
    pool, pool_owner, pool_slot, req_len, query, new_kv, resid, w_uv, w_out, ffn_gain, w_gate, w_up, w_down,
):
    f32, bf = jnp.float32, jnp.bfloat16
    d, tp = lax.axis_index("dp"), lax.axis_index("tp")
    steps, requests, heads, key = query.shape
    width = pool.shape[1]
    swap = [(0, 1), (1, 0), (2, 3), (3, 2)]
    gate_t, up_t = w_gate.T, w_up.T
    gate_o, up_o, down_o = (lax.ppermute(w, "tp", swap) for w in (gate_t, up_t, w_down))

    info = jnp.stack([req_len // width, req_len % width], axis=1).reshape(4).astype(bf)
    info = jnp.broadcast_to(jnp.pad(info, (0, 60))[None], (4 * heads, 64))
    rows = jnp.transpose(query, (1, 0, 2, 3)).reshape(4 * heads, key)
    q_all = gather_dp(jnp.concatenate([rows, info], axis=1), 1)

    codes = q_all[:, 0, key:key + 4].astype(jnp.int32)
    lengths = codes[:, 0::2] * width + codes[:, 1::2]
    member = pool_owner[:, None] == jnp.arange(NDP, dtype=jnp.int32)[None, :]
    own_len = jnp.sum(jnp.where(member[:, :, None], lengths[None], 0), axis=1)
    first_blocks = (own_len[:, 0] + width - 1) // width
    part = (pool_slot >= first_blocks).astype(jnp.int32)
    index = pool_slot - part * first_blocks
    limit = jnp.where(part == 1, own_len[:, 1], own_len[:, 0]) - index * width
    two = jnp.arange(2, dtype=jnp.int32)
    owner = jnp.concatenate([pool_owner, jnp.full((2,), 0, jnp.int32) + d])
    part = jnp.concatenate([part, two])
    lim0 = jnp.concatenate([limit, jnp.full((2,), 1, jnp.int32)])
    lim1 = jnp.concatenate([limit, jnp.full((2,), 2, jnp.int32)])
    slot = owner % 2 * 32 + owner // 2 % 4 * 8 + owner // 8
    new_t = jnp.pad(jnp.transpose(new_kv, (1, 2, 0)), ((0, 0), (0, 0), (0, width - steps)))
    head_part, stats = attend(owner, slot, part, lim0, lim1, q_all, jnp.swapaxes(pool, 1, 2), new_t, w_uv)

    mine = fold_softmax(head_part, stats, 2)
    heads_all = flat_gather_dp(mine, 3)
    head_rows = jnp.transpose(heads_all.reshape(NDP, requests, steps, -1), (2, 0, 1, 3))
    head_rows = head_rows.reshape(steps, NDP * requests, -1)
    partial = jnp.einsum("kc,tnk->tcn", w_out, head_rows, preferred_element_type=f32).astype(bf)
    summed = jnp.sum(swap_tp(partial, 4, True).astype(f32), axis=0)
    attended = (jnp.swapaxes(resid, 1, 2).astype(f32) + summed).astype(bf)

    half = lax.dynamic_index_in_dim(attended, tp % 2, 0, keepdims=False)
    whole = flat_gather_dp(half, 5).reshape(-1, half.shape[1]).astype(f32)
    mean_square = jnp.mean(whole * whole, axis=0, keepdims=True)
    normed = (whole * lax.rsqrt(mean_square + epsilon) * ffn_gain[:, None]).astype(bf)
    both = jnp.dot(
        jnp.concatenate([gate_t, gate_o, up_t, up_o], axis=0), normed, preferred_element_type=f32
    )
    units = both.shape[0] // 2
    hidden = (jax.nn.silu(both[:units]) * both[units:]).astype(bf)
    down = lax.dot_general(
        jnp.concatenate([w_down, down_o], axis=0), hidden, (((0,), (0,)), ((), ())),
        preferred_element_type=f32,
    ).astype(bf)
    cols = half.shape[0]
    summed_cols = fold_sum(down.reshape(NZ, NX, NC, cols, -1), 6)
    share = cols // 4
    pieces = jnp.pad(summed_cols.reshape(4, share, -1), ((0, 0), (0, -share % 8), (0, 0)))
    pieces = swap_tp(pieces, 7, False)[:, :share]
    own = lax.dynamic_slice_in_dim(attended, tp * share, share, 1).astype(f32)
    layer = (own + (pieces[:2] + pieces[2:])).astype(bf)
    return jnp.swapaxes(attended, 1, 2), jnp.swapaxes(layer, 1, 2)


def solution(mesh):
    in_specs = (
        P("dp", None, None),
        P("dp"),
        P("dp"),
        P("dp"),
        P(None, "dp", "tp", None),
        P(None, "dp", None),
        P(None, None, "dp"),
        P("tp", None, None),
        P("tp", "dp"),
        P(),
        P(None, ("dp", "tp")),
        P(None, ("dp", "tp")),
        P(("dp", "tp"), None),
    )
    out_specs = (P(None, None, "dp"), P(None, None, ("dp", "tp")))
    return jax.shard_map(
        per_device, mesh=mesh, in_specs=in_specs, out_specs=out_specs, check_vma=False
    )
```

```python
import functools
import jax
import jax.numpy as jnp
from jax import lax
from jax.experimental import pallas as pl
from jax.experimental.pallas import tpu as pltpu
from jax.sharding import PartitionSpec as P

NZ, NX, NC = 8, 4, 2
NDP = NZ * NX * NC
LOW = -3.0e38
BIG = 56 * 1024 * 1024


def place():
    d = lax.axis_index("dp")
    return lax.div(d, 8), lax.rem(lax.div(d, 2), 4), lax.rem(d, 2), lax.axis_index("tp")


def dp_of(z, x, c):
    return (z * NX + x) * NC + c


def greet(peers):
    barrier = pltpu.get_barrier_semaphore()
    for peer in peers:
        pl.semaphore_signal(barrier, inc=1, device_id=peer, device_id_type=pl.DeviceIdType.MESH)
    pl.semaphore_wait(barrier, len(peers))


def gather_kernel(x_ref, out_ref, send, recv, own_sem):
    z, x, c, tp = place()
    up, down = lax.rem(z + 1, NZ), lax.rem(z + NZ - 1, NZ)
    right, left = lax.rem(x + 1, NX), lax.rem(x + NX - 1, NX)
    to_up, to_down = (dp_of(up, x, c), tp), (dp_of(down, x, c), tp)
    to_right, to_left = (dp_of(z, right, c), tp), (dp_of(z, left, c), tp)
    to_twin = (dp_of(z, x, 1 - c), tp)
    greet((to_up, to_down, to_right, to_left, to_twin))
    me = dp_of(z, x, c)
    started = []

    def push(chunk, peer, own=False):
        copy = pltpu.make_async_remote_copy(
            src_ref=x_ref if own else out_ref.at[chunk],
            dst_ref=out_ref.at[chunk],
            send_sem=send.at[len(started)],
            recv_sem=recv.at[chunk],
            device_id=peer,
            device_id_type=pl.DeviceIdType.MESH,
        )
        copy.start()
        started.append(copy)

    def arrived(chunk):
        pltpu.make_async_remote_copy(
            src_ref=x_ref,
            dst_ref=out_ref.at[chunk],
            send_sem=send.at[0],
            recv_sem=recv.at[chunk],
            device_id=to_twin,
            device_id_type=pl.DeviceIdType.MESH,
        ).wait_recv()

    own_copy = pltpu.make_async_copy(x_ref, out_ref.at[me], own_sem)
    own_copy.start()

    def along_z(step, sign, own=False):
        at = lax.rem(z + NZ - sign * step, NZ)
        chunk = dp_of(at, x, c)
        if not own:
            arrived(chunk)
        if own:
            push(chunk, to_up, own)
            push(chunk, to_down, own)
        elif sign > 0 and step < 4:
            push(chunk, to_up)
        elif sign < 0 and step < 3:
            push(chunk, to_down)
        push(chunk, to_right, own)
        push(chunk, to_left, own)
        push(chunk, to_twin, own)

    def along_x(step, sign):
        at = lax.rem(z + NZ - sign * step, NZ)
        even = step % 2 == 0
        first, second = dp_of(at, left, c), dp_of(at, right, c)
        arrived(first)
        if even:
            push(first, to_right)
        push(first, to_twin)
        arrived(second)
        if not even:
            push(second, to_left)
        push(second, to_twin)

    def across(step, sign):
        at = lax.rem(z + NZ - sign * step, NZ)
        far = dp_of(at, lax.rem(x + 2, NX), c)
        arrived(far)
        push(far, to_twin)

    order = [(0, 1), (1, 1), (1, -1), (2, 1), (2, -1), (3, 1), (3, -1), (4, 1)]
    along_z(0, 1, own=True)
    along_z(1, 1)
    along_z(1, -1)
    for index, (step, sign) in enumerate(order):
        along_x(step, sign)
        if index + 3 < len(order):
            along_z(*order[index + 3])
        if index >= 1:
            across(*order[index - 1])
    across(*order[-1])
    for at_z in range(NZ):
        for at_x in range(NX):
            arrived(dp_of(at_z, at_x, 1 - c))
    own_copy.wait()
    for copy in started:
        copy.wait_send()


def gather_dp(shard, collective_id, space=None):
    space = pl.ANY if space is None else space
    return pl.pallas_call(
        gather_kernel,
        out_shape=jax.ShapeDtypeStruct((NDP,) + shard.shape, shard.dtype),
        in_specs=[pl.BlockSpec(memory_space=space)],
        out_specs=pl.BlockSpec(memory_space=space),
        scratch_shapes=[
            pltpu.SemaphoreType.DMA((63,)),
            pltpu.SemaphoreType.DMA((NDP,)),
            pltpu.SemaphoreType.DMA,
        ],
        compiler_params=pltpu.CompilerParams(
            collective_id=collective_id, has_side_effects=True, vmem_limit_bytes=BIG
        ),
        name="gather_dp",
    )(shard)


def attend_kernel(owner_ref, slot_ref, part_ref, lim0_ref, lim1_ref, q_ref, blk_ref, new_ref, wuv_ref,
                  out_ref, stat_ref, acc, top, tot, table, *, per_step, blocks, heads):
    step = pl.program_id(0)
    rows = 2 * heads
    lat = wuv_ref.shape[1]
    scale = (3 * 64) ** (-0.5)
    width = blk_ref.shape[2]

    @pl.when(step == 0)
    def _():
        def clear(i, _):
            at = pl.multiple_of(i * 128, 128)
            for k in range(lat // 128):
                acc[k, pl.ds(at, 128), :] = jnp.zeros((128, 128), jnp.float32)
            top[pl.ds(at, 128), :] = jnp.full((128, 128), LOW, jnp.float32)
            tot[pl.ds(at, 128), :] = jnp.zeros((128, 128), jnp.float32)
            return 0

        lax.fori_loop(0, acc.shape[1] // 128, clear, 0)

    lane = lax.broadcasted_iota(jnp.int32, (rows, width), 1)
    late = lax.broadcasted_iota(jnp.int32, (rows, width), 0) >= heads

    def look(number, block):
        group, part = owner_ref[number], part_ref[number]
        limit = jnp.where(late, lim1_ref[number], lim0_ref[number])
        both = jnp.dot(q_ref[group, :, :block.shape[0]], block, preferred_element_type=jnp.float32)
        scores = jnp.where(part == 0, both[:rows], both[rows:]) * scale
        keep = lane < limit
        peak = jnp.max(jnp.where(keep, scores, LOW), axis=1, keepdims=True)
        weights = jnp.where(keep, jnp.exp(scores - peak), 0.0)
        mixed = lax.dot_general(
            weights.astype(jnp.bfloat16), block[:lat], (((1,), (1,)), ((), ())),
            preferred_element_type=jnp.float32,
        )
        return peak, jnp.sum(weights, axis=1, keepdims=True), mixed

    def merge(number, found):
        peak, total, mixed = found
        at = pl.multiple_of((slot_ref[number] * 2 + part_ref[number]) * rows, 8)
        old = top[pl.ds(at, rows), :]
        now = jnp.maximum(old, peak)
        fade, gain = jnp.exp(old - now), jnp.exp(peak - now)
        top[pl.ds(at, rows), :] = now
        tot[pl.ds(at, rows), :] = tot[pl.ds(at, rows), :] * fade + total * gain
        for k in range(lat // 128):
            acc[k, pl.ds(at, rows), :] = (
                acc[k, pl.ds(at, rows), :] * fade + mixed[:, k * 128:(k + 1) * 128] * gain)

    found = [look(step * per_step + k, blk_ref[k]) for k in range(per_step)]
    for k in range(per_step):
        merge(step * per_step + k, found[k])

    @pl.when(step == pl.num_programs(0) - 1)
    def _():
        for k in range(2):
            merge(blocks + k, look(blocks + k, new_ref[k]))

        def head(h, _):
            every = pl.ds(h, acc.shape[1] // heads, stride=heads)
            latent = jnp.concatenate([acc[k, every, :] for k in range(lat // 128)], axis=1).astype(jnp.bfloat16)
            table[every, :] = jnp.dot(
                latent, wuv_ref[h], preferred_element_type=jnp.float32)
            return 0

        lax.fori_loop(0, heads, head, 0)
        out_ref[...] = table[...].astype(jnp.bfloat16).reshape(out_ref.shape)
        column = lax.broadcasted_iota(jnp.int32, (2 * rows, 128), 1)

        def gather(j, carry):
            at = pl.multiple_of(j * 2 * rows, 8)
            return (jnp.where(column == j, top[pl.ds(at, 2 * rows), :], carry[0]),
                    jnp.where(column == j, tot[pl.ds(at, 2 * rows), :], carry[1]))

        zero = jnp.zeros((2 * rows, 128), jnp.float32)
        tops, tots = lax.fori_loop(0, NDP, gather, (zero, zero))
        pad = jnp.zeros((128 - 2 * rows, 128), jnp.float32)
        stat_ref[0] = jnp.concatenate([tops, pad], axis=0).T[:NDP]
        stat_ref[1] = jnp.concatenate([tots, pad], axis=0).T[:NDP]


def attend(owner, slot, part, lim0, lim1, q_all, pool_t, new_t, w_uv, per_step=8):
    blocks, key, width = pool_t.shape
    heads, lat, vd = w_uv.shape
    total = NDP * 4 * heads
    vmem = pl.BlockSpec(memory_space=pltpu.VMEM)
    return pl.pallas_call(
        functools.partial(attend_kernel, per_step=per_step, blocks=blocks, heads=heads),
        out_shape=(
            jax.ShapeDtypeStruct((NDP, 4 * heads, vd), jnp.bfloat16),
            jax.ShapeDtypeStruct((2, NDP, 128), jnp.float32),
        ),
        grid_spec=pltpu.PrefetchScalarGridSpec(
            num_scalar_prefetch=5,
            grid=(blocks // per_step,),
            in_specs=[
                vmem,
                pl.BlockSpec((per_step, key, width), lambda i, *_: (i, 0, 0)),
                vmem,
                vmem,
            ],
            out_specs=[vmem, vmem],
            scratch_shapes=[
                pltpu.VMEM((lat // 128, total, 128), jnp.float32),
                pltpu.VMEM((total, 128), jnp.float32),
                pltpu.VMEM((total, 128), jnp.float32),
                pltpu.VMEM((total, vd), jnp.float32),
            ],
        ),
        compiler_params=pltpu.CompilerParams(vmem_limit_bytes=BIG, dimension_semantics=("arbitrary",)),
        name="attend",
    )(owner, slot, part, lim0, lim1, q_all, pool_t, new_t, w_uv)


def columns_of(rows):
    count = rows.shape[0]
    if count < 128:
        rows = jnp.concatenate([rows, jnp.zeros((128 - count, 128), jnp.float32)], axis=0)
    return rows.T


def tail_kernel(h_ref, st_ref, wo_ref, res_ref, gain_ref, g0_ref, g1_ref, u0_ref, u1_ref, d0_ref, d1_ref,
                att_ref, lay_ref,
                c_buf, c_st, mine, m_st, x_buf, x_st, z_src, z_st, z_buf, z_in,
                h_all, h_flat, y_buf, a_all, normed, w_all, d_cols, down, dc_buf, d_mine, dx_buf, dz_src, dz_buf,
                y_out, y_in, send, recv):
    f32, bf = jnp.float32, jnp.bfloat16
    z, x, c, tp = place()
    z_off, x_off, x_back = (1, 7, 2, 6, 3, 5, 4), (1, 3, 2), (3, 1, 2)
    z_peers = [lax.rem(z + k, NZ) for k in z_off]
    x_peers = [lax.rem(x + k, NX) for k in x_off]
    y_peers = [lax.rem(tp + k, 4) for k in x_off]
    me = dp_of(z, x, c)
    twin = (dp_of(z, x, 1 - c), tp)
    greet(
        [(dp_of(k, x, c), tp) for k in z_peers] + [(dp_of(z, k, c), tp) for k in x_peers]
        + [(me, k) for k in y_peers] + [twin]
    )
    used = []

    def remote(src, dst, peer):
        copy = pltpu.make_async_remote_copy(
            src_ref=src, dst_ref=dst, send_sem=send.at[len(used)], recv_sem=recv.at[len(used)],
            device_id=peer, device_id_type=pl.DeviceIdType.MESH,
        )
        used.append(copy)
        copy.start()
        return copy

    def finish(copies):
        for copy in copies:
            copy.wait()

    half = NDP // 2
    there = pl.multiple_of((1 - c) * half, half)
    here = pl.multiple_of(c * half, half)
    copies = [
        remote(h_ref.at[pl.ds(there, half)], c_buf, twin),
        remote(st_ref.at[:, pl.ds(there, half)], c_st, twin),
    ]
    units = g0_ref.shape[0]
    pad = w_all.shape[0] // 4
    width = w_all.shape[1]
    for k, ref in enumerate((g0_ref, g1_ref, u0_ref, u1_ref)):
        w_all[k * pad:(k + 1) * pad, :] = jnp.concatenate(
            [ref[...], jnp.zeros((pad - units, width), bf)], axis=0)
    finish(copies)

    def merge(stats):
        tops = stats[0][0]
        for s in stats[1:]:
            tops = jnp.maximum(tops, s[0])
        factors = [jnp.exp(s[0] - tops) for s in stats]
        total = sum(f * s[1] for f, s in zip(factors, stats))
        return tops, total, [columns_of(f) for f in factors]

    rows = h_ref.shape[1]
    tops, total, columns = merge([st_ref[:, pl.ds(here, half), :], c_st[...]])
    m_st[0] = tops
    m_st[1] = total
    for j in range(half):
        mine[j] = (
            h_ref[here + j].astype(f32) * columns[0][:rows, j:j + 1]
            + c_buf[j].astype(f32) * columns[1][:rows, j:j + 1]
        ).astype(bf)
    copies = []
    for k, peer in enumerate(x_peers):
        at = pl.multiple_of(peer * NZ, NZ)
        dst = (dp_of(z, peer, c), tp)
        copies.append(remote(mine.at[pl.ds(at, NZ)], x_buf.at[k], dst))
        copies.append(remote(m_st.at[:, pl.ds(at, NZ)], x_st.at[k], dst))
    for k in range(width // 128):
        block = jnp.concatenate(
            [d0_ref[:, k * 128:(k + 1) * 128].astype(f32), jnp.zeros((pad - units, 128), f32),
             d1_ref[:, k * 128:(k + 1) * 128].astype(f32), jnp.zeros((128 - pad - units, 128), f32)], axis=0)
        d_cols[k * 128:(k + 1) * 128, :] = block.T.astype(bf)
    finish(copies)
    at = pl.multiple_of(x * NZ, NZ)
    tops, total, columns = merge([m_st[:, pl.ds(at, NZ), :]] + [x_st[k] for k in range(3)])
    for j in range(NZ):
        z_src[j] = (
            mine[at + j].astype(f32) * columns[0][:rows, j:j + 1]
            + sum(x_buf[k, j].astype(f32) * columns[k + 1][:rows, j:j + 1] for k in range(3))
        ).astype(bf)
        z_st[j, 0:1, :] = tops[j:j + 1]
        z_st[j, 1:2, :] = total[j:j + 1]
        z_st[j, 2:8, :] = jnp.zeros((6, 128), f32)
    copies = []
    for k, peer in enumerate(z_peers):
        dst = (dp_of(peer, x, c), tp)
        copies.append(remote(z_src.at[peer], z_buf.at[k], dst))
        copies.append(remote(z_st.at[peer], z_in.at[k], dst))
    finish(copies)
    stats = [z_st[z]] + [z_in[k] for k in range(7)]
    tops = jnp.concatenate([s[0:1] for s in stats], axis=0)
    tots = jnp.concatenate([s[1:2] for s in stats], axis=0)
    factor = jnp.exp(tops - jnp.max(tops, axis=0, keepdims=True))
    columns = columns_of(factor / jnp.sum(factor * tots, axis=0, keepdims=True))
    final = z_src[z].astype(f32) * columns[:rows, 0:1]
    for k in range(7):
        final = final + z_buf[k].astype(f32) * columns[:rows, k + 1:k + 2]

    def gather(buf):
        first = [remote(buf.at[z, x, c], buf.at[z, x, c], (dp_of(peer, x, c), tp)) for peer in z_peers]
        for copy in first:
            copy.wait_recv()
        second = [
            remote(buf.at[:, x, c], buf.at[:, x, c], (dp_of(z, peer, c), tp)) for peer in x_peers
        ]
        third = [remote(buf.at[:, x, c], buf.at[:, x, c], twin)]
        for k, copy in enumerate(second):
            copy.wait_recv()
            at = lax.rem(x + x_back[k], NX)
            third.append(remote(buf.at[:, at, c], buf.at[:, at, c], twin))
        for copy in third:
            copy.wait_recv()
        for copy in first + second + third:
            copy.wait_send()

    h_all[z, x, c] = final.astype(bf)
    gather(h_all)
    everyone = [(i, j, k) for i in range(NZ) for j in range(NX) for k in range(NC)]
    for n, (i, j, k) in enumerate(everyone):
        h_flat[n * rows:(n + 1) * rows, :] = h_all[i, j, k].astype(f32)
    heads = rows // 4
    for t in range(2):
        value = jnp.zeros(att_ref.shape[1:], f32)
        for h in range(0, heads, 2):
            both = jnp.concatenate(
                [h_flat[pl.ds(t * heads + h + k, 128, stride=rows // 2), :].astype(bf) for k in range(2)], axis=1)
            value = value + lax.dot_general(
                wo_ref[:, h * 128:(h + 2) * 128], both, (((1,), (1,)), ((), ())), preferred_element_type=f32)
        y_buf[tp, t] = value.astype(bf)
    finish([remote(y_buf.at[tp], y_buf.at[tp], (me, peer)) for peer in y_peers])
    attended = []
    for t in range(2):
        value = res_ref[t].astype(f32) + sum(y_buf[k, t].astype(f32) for k in range(4))
        attended.append(value.astype(bf))
        att_ref[t] = attended[t]
    odd = lax.rem(tp, 2)
    a_all[z, x, c] = jnp.where(odd == 0, attended[0].astype(f32), attended[1].astype(f32)).astype(bf)
    gather(a_all)

    cols = att_ref.shape[1]
    square = jnp.zeros((8, 128), f32)
    for i, j, k in everyone:
        part = a_all[i, j, k].astype(f32)
        square = square + jnp.sum((part * part).reshape(cols // 8, 8, 128), axis=0)
    inverse = lax.rsqrt(jnp.sum(square, axis=0, keepdims=True) / width + 1e-6)
    gains = columns_of(gain_ref[...])
    for n, (i, j, k) in enumerate(everyone):
        normed[n * cols:(n + 1) * cols, :] = (
            a_all[i, j, k].astype(f32) * inverse * gains[:cols, n:n + 1]).astype(bf)

    def product(i, total):
        at = pl.multiple_of(i * 512, 512)
        return total + jnp.dot(
            w_all[:, pl.ds(at, 512)], normed[pl.ds(at, 512), :], preferred_element_type=f32)

    both = lax.fori_loop(0, width // 512, product, jnp.zeros((4 * pad, 128), f32))
    gate, up = both[:2 * pad], both[2 * pad:]
    hidden = (gate / (1.0 + jnp.exp(-gate)) * up).astype(bf)
    hidden = jnp.concatenate([hidden, jnp.zeros((128 - 2 * pad, 128), bf)], axis=0)

    def piece(n):
        at = pl.multiple_of((lax.rem(n, NZ) * 8 + lax.rem(lax.div(n, NZ), NX) * 2 + lax.div(n, half)) * cols, 16)
        return jnp.dot(d_cols[pl.ds(at, cols), :], hidden, preferred_element_type=f32)

    copies = []
    for k in range(2):
        for i in range(16):
            down[k * 16 + i] = piece(there + k * 16 + i).astype(bf)
        copies.append(remote(down.at[pl.ds(k * 16, 16)], dc_buf.at[pl.ds(k * 16, 16)], twin))
    finish(copies)
    copies = []
    for k, peer in enumerate(x_peers):
        for i in range(NZ):
            n = peer * NZ + i
            d_mine[n] = (piece(here + n) + dc_buf[n].astype(f32)).astype(bf)
        at = pl.multiple_of(peer * NZ, NZ)
        copies.append(remote(d_mine.at[pl.ds(at, NZ)], dx_buf.at[k], (dp_of(z, peer, c), tp)))
    finish(copies)

    def meet(at):
        n = x * NZ + at
        return piece(here + n) + dc_buf[n].astype(f32) + sum(dx_buf[k, at].astype(f32) for k in range(3))

    copies = []
    for k, peer in enumerate(z_peers):
        dz_src[k] = meet(peer).astype(bf)
        copies.append(remote(dz_src.at[k], dz_buf.at[k], (dp_of(peer, x, c), tp)))
    final = meet(z)
    finish(copies)
    for k in range(7):
        final = final + dz_buf[k].astype(f32)
    share = cols // 4
    empty = jnp.zeros((y_out.shape[1] - share, 128), f32)
    for k in range(4):
        y_out[k] = jnp.concatenate([final[k * share:(k + 1) * share], empty], axis=0)
    y_in[tp] = y_out[tp]
    finish([remote(y_out.at[peer], y_in.at[tp], (me, peer)) for peer in y_peers])
    for t in range(2):
        own = attended[t].astype(f32)
        base = own[:share]
        for k in range(1, 4):
            base = jnp.where(tp == k, own[k * share:(k + 1) * share], base)
        lay_ref[t] = (base + (y_in[t] + y_in[t + 2])[:share]).astype(bf)


def tail(h, st, wo, res, gain, g0, g1, u0, u1, d0, d1, collective_id):
    vmem = pl.BlockSpec(memory_space=pltpu.VMEM)
    _, rows, vd = h.shape
    cols, width = wo.shape[0], g0.shape[1]
    bf, f32 = jnp.bfloat16, jnp.float32
    pad = -(-g0.shape[0] // 16) * 16
    share = cols // 4
    tall = -(-share // 8) * 8
    shapes = [
        ((32, rows, vd), bf), ((2, 32, 128), f32), ((32, rows, vd), bf), ((2, 32, 128), f32),
        ((3, NZ, rows, vd), bf), ((3, 2, NZ, 128), f32), ((NZ, rows, vd), bf), ((NZ, 8, 128), f32),
        ((7, rows, vd), bf), ((7, 8, 128), f32),
        ((NZ, NX, NC, rows, vd), bf), ((NDP * rows, vd), f32), ((4,) + res.shape, bf),
        ((NZ, NX, NC, cols, 128), bf), ((width, 128), bf), ((4 * pad, width), bf), ((width, 128), bf),
        ((32, cols, 128), bf), ((32, cols, 128), bf), ((32, cols, 128), bf), ((3, NZ, cols, 128), bf),
        ((7, cols, 128), bf), ((7, cols, 128), bf), ((4, tall, 128), f32), ((4, tall, 128), f32),
    ]
    return pl.pallas_call(
        tail_kernel,
        out_shape=(
            jax.ShapeDtypeStruct(res.shape, bf),
            jax.ShapeDtypeStruct((2, share, 128), bf),
        ),
        in_specs=[vmem] * 11,
        out_specs=(vmem, vmem),
        scratch_shapes=[pltpu.VMEM(shape, kind) for shape, kind in shapes]
        + [pltpu.SemaphoreType.DMA((72,)), pltpu.SemaphoreType.DMA((72,))],
        compiler_params=pltpu.CompilerParams(
            collective_id=collective_id, has_side_effects=True, vmem_limit_bytes=BIG),
        name="tail",
    )(h, st, wo, res, gain, g0, g1, u0, u1, d0, d1)


def per_device(
    pool, pool_owner, pool_slot, req_len, query, new_kv, resid, w_uv, w_out, ffn_gain, w_gate, w_up, w_down,
):
    bf = jnp.bfloat16
    d = lax.axis_index("dp")
    steps, requests, heads, key = query.shape
    width = pool.shape[1]
    swap = [(0, 1), (1, 0), (2, 3), (3, 2)]
    gate_t, up_t = w_gate.T, w_up.T
    gate_o, up_o, down_o = (lax.ppermute(w, "tp", swap) for w in (gate_t, up_t, w_down))

    info = jnp.stack([req_len // width, req_len % width], axis=1).reshape(4).astype(bf)
    info = jnp.broadcast_to(jnp.pad(info, (0, 60))[None], (4 * heads, 64))
    rows = jnp.transpose(query, (1, 0, 2, 3)).reshape(4 * heads, key)
    q_all = gather_dp(jnp.concatenate([rows, info], axis=1), 1)

    codes = q_all[:, 0, key:key + 4].astype(jnp.int32)
    lengths = codes[:, 0::2] * width + codes[:, 1::2]
    member = pool_owner[:, None] == jnp.arange(NDP, dtype=jnp.int32)[None, :]
    own_len = jnp.sum(jnp.where(member[:, :, None], lengths[None], 0), axis=1)
    first_blocks = (own_len[:, 0] + width - 1) // width
    part = (pool_slot >= first_blocks).astype(jnp.int32)
    index = pool_slot - part * first_blocks
    limit = jnp.where(part == 1, own_len[:, 1], own_len[:, 0]) - index * width
    two = jnp.arange(2, dtype=jnp.int32)
    owner = jnp.concatenate([pool_owner, jnp.full((2,), 0, jnp.int32) + d])
    part = jnp.concatenate([part, two])
    lim0 = jnp.concatenate([limit, jnp.full((2,), 1, jnp.int32)])
    lim1 = jnp.concatenate([limit, jnp.full((2,), 2, jnp.int32)])
    slot = owner % 2 * 32 + owner // 2 % 4 * 8 + owner // 8
    new_t = jnp.pad(jnp.transpose(new_kv, (1, 2, 0)), ((0, 0), (0, 0), (0, width - steps)))
    head_part, stats = attend(owner, slot, part, lim0, lim1, q_all, jnp.swapaxes(pool, 1, 2), new_t, w_uv)

    cols = resid.shape[2]
    gain = jnp.pad(ffn_gain.reshape(NDP, cols), ((0, 0), (0, 128 - cols)))
    attended, layer = tail(
        head_part, stats, w_out.T, jnp.swapaxes(resid, 1, 2), gain, gate_t, gate_o, up_t, up_o, w_down, down_o, 2
    )
    return jnp.swapaxes(attended, 1, 2), jnp.swapaxes(layer, 1, 2)


def solution(mesh):
    in_specs = (
        P("dp", None, None),
        P("dp"),
        P("dp"),
        P("dp"),
        P(None, "dp", "tp", None),
        P(None, "dp", None),
        P(None, None, "dp"),
        P("tp", None, None),
        P("tp", "dp"),
        P(),
        P(None, ("dp", "tp")),
        P(None, ("dp", "tp")),
        P(("dp", "tp"), None),
    )
    out_specs = (P(None, None, "dp"), P(None, None, ("dp", "tp")))
    return jax.shard_map(
        per_device, mesh=mesh, in_specs=in_specs, out_specs=out_specs, check_vma=False
    )
```

```python
import functools
import jax
import jax.numpy as jnp
from jax import lax
from jax.experimental import pallas as pl
from jax.experimental.pallas import tpu as pltpu
from jax.sharding import PartitionSpec as P

NZ, NX, NC = 8, 4, 2
NDP = NZ * NX * NC
LOW = -3.0e38
BIG = 56 * 1024 * 1024


def place():
    d = lax.axis_index("dp")
    return lax.div(d, 8), lax.rem(lax.div(d, 2), 4), lax.rem(d, 2), lax.axis_index("tp")


def dp_of(z, x, c):
    return (z * NX + x) * NC + c


def greet(peers):
    barrier = pltpu.get_barrier_semaphore()
    for peer in peers:
        pl.semaphore_signal(barrier, inc=1, device_id=peer, device_id_type=pl.DeviceIdType.MESH)
    pl.semaphore_wait(barrier, len(peers))


def gather_kernel(x_ref, out_ref, send, recv, own_sem, *, cut):
    z, x, c, tp = place()
    up, down = lax.rem(z + 1, NZ), lax.rem(z + NZ - 1, NZ)
    right, left = lax.rem(x + 1, NX), lax.rem(x + NX - 1, NX)
    to_up, to_down = (dp_of(up, x, c), tp), (dp_of(down, x, c), tp)
    to_right, to_left = (dp_of(z, right, c), tp), (dp_of(z, left, c), tp)
    to_twin = (dp_of(z, x, 1 - c), tp)
    greet((to_up, to_down, to_right, to_left, to_twin))
    me = dp_of(z, x, c)
    spans = (pl.ds(0, cut), pl.ds(cut, x_ref.shape[0] - cut))
    started = []

    def push(chunk, part, peer, own=False):
        copy = pltpu.make_async_remote_copy(
            src_ref=x_ref.at[spans[part]] if own else out_ref.at[chunk, spans[part]],
            dst_ref=out_ref.at[chunk, spans[part]],
            send_sem=send.at[len(started)],
            recv_sem=recv.at[part, chunk],
            device_id=peer,
            device_id_type=pl.DeviceIdType.MESH,
        )
        copy.start()
        started.append(copy)

    def arrived(chunk, part):
        pltpu.make_async_remote_copy(
            src_ref=x_ref.at[spans[part]],
            dst_ref=out_ref.at[chunk, spans[part]],
            send_sem=send.at[0],
            recv_sem=recv.at[part, chunk],
            device_id=to_twin,
            device_id_type=pl.DeviceIdType.MESH,
        ).wait_recv()

    def handle(part, kz, kx):
        own = kz == 0 and kx == 0
        chunk = me if own else dp_of(lax.rem(z + NZ - kz, NZ), lax.rem(x + NX - kx, NX), c)
        if not own:
            arrived(chunk, part)
        reach_up = 4 if part == 0 or kx % 2 == 0 else 3
        reach_down = reach_up - 7
        reach_right = 2 if kz % 2 == 0 else 1
        reach_left = reach_right - 3
        if part == 0:
            along_z, along_x = kx == 0, True
        else:
            along_z, along_x = True, kz == 0
        if along_z and 0 <= kz < reach_up:
            push(chunk, part, to_up, own)
        if along_z and reach_down < kz <= 0:
            push(chunk, part, to_down, own)
        if along_x and 0 <= kx < reach_right:
            push(chunk, part, to_right, own)
        if along_x and reach_left < kx <= 0:
            push(chunk, part, to_left, own)
        push(chunk, part, to_twin, own)

    events = []
    for part in range(2):
        for a in range(NZ):
            for b in range(NX):
                odd_b, odd_a = b % 2 == 1, a % 2 == 1
                kz = a if a <= (4 if part == 0 or not odd_b else 3) else a - NZ
                kx = b if b <= (2 if not odd_a else 1) else b - NX
                first, second = (abs(kz), abs(kx)) if part == 0 else (abs(kx), abs(kz))
                events.append((first + second, second, part, kz, kx))
    own_copy = pltpu.make_async_copy(x_ref, out_ref.at[me], own_sem)
    own_copy.start()
    for _, _, part, kz, kx in sorted(events):
        handle(part, kz, kx)
    for at_z in range(NZ):
        for at_x in range(NX):
            for part in range(2):
                arrived(dp_of(at_z, at_x, 1 - c), part)
    own_copy.wait()
    for copy in started:
        copy.wait_send()


def gather_dp(shard, collective_id, space=None, cut=48):
    space = pl.ANY if space is None else space
    return pl.pallas_call(
        functools.partial(gather_kernel, cut=cut),
        out_shape=jax.ShapeDtypeStruct((NDP,) + shard.shape, shard.dtype),
        in_specs=[pl.BlockSpec(memory_space=space)],
        out_specs=pl.BlockSpec(memory_space=space),
        scratch_shapes=[
            pltpu.SemaphoreType.DMA((126,)),
            pltpu.SemaphoreType.DMA((2, NDP)),
            pltpu.SemaphoreType.DMA,
        ],
        compiler_params=pltpu.CompilerParams(
            collective_id=collective_id, has_side_effects=True, vmem_limit_bytes=4 * 1024 * 1024
        ),
        name="gather_dp",
    )(shard)


def attend_kernel(owner_ref, slot_ref, part_ref, lim0_ref, lim1_ref, q_ref, blk_ref, new_ref, wuv_ref,
                  out_ref, stat_ref, acc, top, tot, table, *, per_step, blocks, heads):
    step = pl.program_id(0)
    rows = 2 * heads
    lat = wuv_ref.shape[1]
    scale = (3 * 64) ** (-0.5)
    width = blk_ref.shape[2]

    @pl.when(step == 0)
    def _():
        def clear(i, _):
            at = pl.multiple_of(i * 128, 128)
            for k in range(lat // 128):
                acc[k, pl.ds(at, 128), :] = jnp.zeros((128, 128), jnp.float32)
            top[pl.ds(at, 128), :] = jnp.full((128, 128), LOW, jnp.float32)
            tot[pl.ds(at, 128), :] = jnp.zeros((128, 128), jnp.float32)
            return 0

        lax.fori_loop(0, acc.shape[1] // 128, clear, 0)

    lane = lax.broadcasted_iota(jnp.int32, (rows, width), 1)
    late = lax.broadcasted_iota(jnp.int32, (rows, width), 0) >= heads

    def look(number, block):
        group, part = owner_ref[number], part_ref[number]
        limit = jnp.where(late, lim1_ref[number], lim0_ref[number])
        both = jnp.dot(q_ref[group, :, :block.shape[0]], block, preferred_element_type=jnp.float32)
        scores = jnp.where(part == 0, both[:rows], both[rows:]) * scale
        keep = lane < limit
        peak = jnp.max(jnp.where(keep, scores, LOW), axis=1, keepdims=True)
        weights = jnp.where(keep, jnp.exp(scores - peak), 0.0)
        mixed = lax.dot_general(
            weights.astype(jnp.bfloat16), block[:lat], (((1,), (1,)), ((), ())),
            preferred_element_type=jnp.float32,
        )
        return peak, jnp.sum(weights, axis=1, keepdims=True), mixed

    def merge(number, found):
        peak, total, mixed = found
        at = pl.multiple_of((slot_ref[number] * 2 + part_ref[number]) * rows, 8)
        old = top[pl.ds(at, rows), :]
        now = jnp.maximum(old, peak)
        fade, gain = jnp.exp(old - now), jnp.exp(peak - now)
        top[pl.ds(at, rows), :] = now
        tot[pl.ds(at, rows), :] = tot[pl.ds(at, rows), :] * fade + total * gain
        for k in range(lat // 128):
            acc[k, pl.ds(at, rows), :] = (
                acc[k, pl.ds(at, rows), :] * fade + mixed[:, k * 128:(k + 1) * 128] * gain)

    found = [look(step * per_step + k, blk_ref[k]) for k in range(per_step)]
    for k in range(per_step):
        merge(step * per_step + k, found[k])

    @pl.when(step == pl.num_programs(0) - 1)
    def _():
        for k in range(2):
            merge(blocks + k, look(blocks + k, new_ref[k]))

        def head(h, _):
            every = pl.ds(h, acc.shape[1] // heads, stride=heads)
            latent = jnp.concatenate([acc[k, every, :] for k in range(lat // 128)], axis=1).astype(jnp.bfloat16)
            table[every, :] = jnp.dot(
                latent, wuv_ref[h], preferred_element_type=jnp.float32)
            return 0

        lax.fori_loop(0, heads, head, 0)
        out_ref[...] = table[...].astype(jnp.bfloat16).reshape(out_ref.shape)
        column = lax.broadcasted_iota(jnp.int32, (2 * rows, 128), 1)

        def gather(j, carry):
            at = pl.multiple_of(j * 2 * rows, 8)
            return (jnp.where(column == j, top[pl.ds(at, 2 * rows), :], carry[0]),
                    jnp.where(column == j, tot[pl.ds(at, 2 * rows), :], carry[1]))

        zero = jnp.zeros((2 * rows, 128), jnp.float32)
        tops, tots = lax.fori_loop(0, NDP, gather, (zero, zero))
        pad = jnp.zeros((128 - 2 * rows, 128), jnp.float32)
        stat_ref[0] = jnp.concatenate([tops, pad], axis=0).T[:NDP]
        stat_ref[1] = jnp.concatenate([tots, pad], axis=0).T[:NDP]


def attend(owner, slot, part, lim0, lim1, q_all, pool_t, new_t, w_uv, per_step=8):
    blocks, key, width = pool_t.shape
    heads, lat, vd = w_uv.shape
    total = NDP * 4 * heads
    vmem = pl.BlockSpec(memory_space=pltpu.VMEM)
    return pl.pallas_call(
        functools.partial(attend_kernel, per_step=per_step, blocks=blocks, heads=heads),
        out_shape=(
            jax.ShapeDtypeStruct((NDP, 4 * heads, vd), jnp.bfloat16),
            jax.ShapeDtypeStruct((2, NDP, 128), jnp.float32),
        ),
        grid_spec=pltpu.PrefetchScalarGridSpec(
            num_scalar_prefetch=5,
            grid=(blocks // per_step,),
            in_specs=[
                vmem,
                pl.BlockSpec((per_step, key, width), lambda i, *_: (i, 0, 0)),
                vmem,
                vmem,
            ],
            out_specs=[vmem, vmem],
            scratch_shapes=[
                pltpu.VMEM((lat // 128, total, 128), jnp.float32),
                pltpu.VMEM((total, 128), jnp.float32),
                pltpu.VMEM((total, 128), jnp.float32),
                pltpu.VMEM((total, vd), jnp.float32),
            ],
        ),
        compiler_params=pltpu.CompilerParams(vmem_limit_bytes=36 * 1024 * 1024, dimension_semantics=("arbitrary",)),
        name="attend",
    )(owner, slot, part, lim0, lim1, q_all, pool_t, new_t, w_uv)


def columns_of(rows):
    count = rows.shape[0]
    if count < 128:
        rows = jnp.concatenate([rows, jnp.zeros((128 - count, 128), jnp.float32)], axis=0)
    return rows.T


def tail_kernel(h_ref, st_ref, wo_ref, res_ref, gain_ref, g0_ref, g1_ref, u0_ref, u1_ref, d0_ref, d1_ref,
                att_ref, lay_ref,
                c_buf, c_st, mine, m_st, x_buf, x_st, z_src, z_st, z_buf, z_in,
                h_all, h_flat, y_buf, a_all, normed, w_all, d_cols, down, dc_buf, d_mine, dx_buf, dz_src, dz_buf,
                y_out, y_in, send, recv):
    f32, bf = jnp.float32, jnp.bfloat16
    z, x, c, tp = place()
    z_off, x_off, x_back = (1, 7, 2, 6, 3, 5, 4), (1, 3, 2), (3, 1, 2)
    z_peers = [lax.rem(z + k, NZ) for k in z_off]
    x_peers = [lax.rem(x + k, NX) for k in x_off]
    y_peers = [lax.rem(tp + k, 4) for k in x_off]
    me = dp_of(z, x, c)
    twin = (dp_of(z, x, 1 - c), tp)
    greet(
        [(dp_of(k, x, c), tp) for k in z_peers] + [(dp_of(z, k, c), tp) for k in x_peers]
        + [(me, k) for k in y_peers] + [twin]
    )
    used = []

    def remote(src, dst, peer):
        copy = pltpu.make_async_remote_copy(
            src_ref=src, dst_ref=dst, send_sem=send.at[len(used)], recv_sem=recv.at[len(used)],
            device_id=peer, device_id_type=pl.DeviceIdType.MESH,
        )
        used.append(copy)
        copy.start()
        return copy

    def finish(copies):
        for copy in copies:
            copy.wait()

    half = NDP // 2
    there = pl.multiple_of((1 - c) * half, half)
    here = pl.multiple_of(c * half, half)
    far_first = [lax.rem(z + k, NZ) for k in (4, 3, 5, 2, 6, 1, 7, 0)]
    far_index = (4, 3, 5, 2, 6, 1, 7, 0)
    stat_copy = remote(st_ref.at[:, pl.ds(there, half)], c_st, twin)
    c_copies = [remote(h_ref.at[1 - c, :, zz], c_buf.at[:, zz], twin) for zz in far_first]
    units = g0_ref.shape[0]
    pad = w_all.shape[0] // 4
    width = w_all.shape[1]
    for k, ref in enumerate((g0_ref, g1_ref, u0_ref, u1_ref)):
        w_all[k * pad:(k + 1) * pad, :] = jnp.concatenate(
            [ref[...], jnp.zeros((pad - units, width), bf)], axis=0)
    stat_copy.wait()

    def relative(full):
        full = pltpu.roll(full, lax.rem(half - x * NZ, half), 0)
        return jnp.concatenate(
            [pltpu.roll(full[k * NZ:(k + 1) * NZ], lax.rem(NZ - z, NZ), 0) for k in range(NX)], axis=0)

    def merge(stats):
        tops = stats[0][0]
        for s in stats[1:]:
            tops = jnp.maximum(tops, s[0])
        factors = [jnp.exp(s[0] - tops) for s in stats]
        total = sum(f * s[1] for f, s in zip(factors, stats))
        return tops, total, [columns_of(f) for f in factors]

    rows = h_ref.shape[3]
    tops, total, columns = merge([
        [relative(st_ref[k, pl.ds(here, half), :]) for k in range(2)],
        [relative(c_st[k]) for k in range(2)],
    ])
    m_st[0] = tops
    m_st[1] = total
    x_stats = [
        remote(m_st.at[:, pl.ds(shift * NZ, NZ)], x_st.at[k], (dp_of(z, peer, c), tp))
        for k, (shift, peer) in enumerate(zip(x_off, x_peers))
    ]
    x_all = [x] + x_peers
    x_copies = []
    for zi, zz, c_copy in zip(far_index, far_first, c_copies):
        c_copy.wait()
        sent = []
        for k, peer in enumerate(x_all):
            n = (0, *x_off)[k] * NZ + zi
            mine[peer, zz] = (
                h_ref[c, peer, zz].astype(f32) * columns[0][:rows, n:n + 1]
                + c_buf[peer, zz].astype(f32) * columns[1][:rows, n:n + 1]
            ).astype(bf)
            if k > 0:
                sent.append(remote(mine.at[peer, zz], x_buf.at[k - 1, zz], (dp_of(z, peer, c), tp)))
        x_copies.append(sent)
    for k in range(width // 128):
        block = jnp.concatenate(
            [d0_ref[:, k * 128:(k + 1) * 128].astype(f32), jnp.zeros((pad - units, 128), f32),
             d1_ref[:, k * 128:(k + 1) * 128].astype(f32), jnp.zeros((128 - pad - units, 128), f32)], axis=0)
        d_cols[k * 128:(k + 1) * 128, :] = block.T.astype(bf)
    finish(x_stats)
    tops, total, columns = merge([m_st[:, 0:NZ, :]] + [x_st[k] for k in range(3)])
    copies = []
    for zi, zz, sent in zip(far_index, far_first, x_copies):
        finish(sent)
        z_src[zz] = (
            mine[x, zz].astype(f32) * columns[0][:rows, zi:zi + 1]
            + sum(x_buf[k, zz].astype(f32) * columns[k + 1][:rows, zi:zi + 1] for k in range(3))
        ).astype(bf)
        z_st[zz, 0:1, :] = tops[zi:zi + 1]
        z_st[zz, 1:2, :] = total[zi:zi + 1]
        z_st[zz, 2:8, :] = jnp.zeros((6, 128), f32)
        if zi > 0:
            dst = (dp_of(zz, x, c), tp)
            copies.append(remote(z_st.at[zz], z_in.at[zi - 1], dst))
            copies.append(remote(z_src.at[zz], z_buf.at[zi - 1], dst))
    finish(copies)
    stats = [z_st[z]] + [z_in[k] for k in range(7)]
    tops = jnp.concatenate([s[0:1] for s in stats], axis=0)
    tots = jnp.concatenate([s[1:2] for s in stats], axis=0)
    factor = jnp.exp(tops - jnp.max(tops, axis=0, keepdims=True))
    columns = columns_of(factor / jnp.sum(factor * tots, axis=0, keepdims=True))
    final = z_src[z].astype(f32) * columns[:rows, 0:1]
    for k in range(7):
        final = final + z_buf[k].astype(f32) * columns[:rows, k + 1:k + 2]

    def gather(buf):
        def ahead(zz, peer):
            return remote(buf.at[zz, x, c], buf.at[zz, x, c], (dp_of(z, peer, c), tp))

        first = [remote(buf.at[z, x, c], buf.at[z, x, c], (dp_of(peer, x, c), tp)) for peer in z_peers]
        second = [[ahead(z, peer)] for peer in x_peers]
        for k, copy in enumerate(first):
            copy.wait_recv()
            for row, peer in zip(second, x_peers):
                row.append(ahead(lax.rem(z + NZ - z_off[k], NZ), peer))
        third = [remote(buf.at[:, x, c], buf.at[:, x, c], twin)]
        for k, row in enumerate(second):
            for copy in row:
                copy.wait_recv()
            at = lax.rem(x + x_back[k], NX)
            third.append(remote(buf.at[:, at, c], buf.at[:, at, c], twin))
        for copy in third:
            copy.wait_recv()
        for copy in first + sum(second, []) + third:
            copy.wait_send()

    h_all[z, x, c] = final.astype(bf)
    gather(h_all)
    everyone = [(i, j, k) for i in range(NZ) for j in range(NX) for k in range(NC)]
    for n, (i, j, k) in enumerate(everyone):
        h_flat[n * rows:(n + 1) * rows, :] = h_all[i, j, k].astype(f32)
    heads = rows // 4
    for t in range(2):
        value = jnp.zeros(att_ref.shape[1:], f32)
        for h in range(0, heads, 2):
            both = jnp.concatenate(
                [h_flat[pl.ds(t * heads + h + k, 128, stride=rows // 2), :].astype(bf) for k in range(2)], axis=1)
            value = value + lax.dot_general(
                wo_ref[:, h * 128:(h + 2) * 128], both, (((1,), (1,)), ((), ())), preferred_element_type=f32)
        y_buf[tp, t] = value.astype(bf)
    finish([remote(y_buf.at[tp], y_buf.at[tp], (me, peer)) for peer in y_peers])
    attended = []
    for t in range(2):
        value = res_ref[t].astype(f32) + sum(y_buf[k, t].astype(f32) for k in range(4))
        attended.append(value.astype(bf))
        att_ref[t] = attended[t]
    odd = lax.rem(tp, 2)
    a_all[z, x, c] = jnp.where(odd == 0, attended[0].astype(f32), attended[1].astype(f32)).astype(bf)
    gather(a_all)

    cols = att_ref.shape[1]
    square = jnp.zeros((8, 128), f32)
    for i, j, k in everyone:
        part = a_all[i, j, k].astype(f32)
        square = square + jnp.sum((part * part).reshape(cols // 8, 8, 128), axis=0)
    inverse = lax.rsqrt(jnp.sum(square, axis=0, keepdims=True) / width + 1e-6)
    gains = columns_of(gain_ref[...])
    for n, (i, j, k) in enumerate(everyone):
        normed[n * cols:(n + 1) * cols, :] = (
            a_all[i, j, k].astype(f32) * inverse * gains[:cols, n:n + 1]).astype(bf)

    def product(i, total):
        at = pl.multiple_of(i * 512, 512)
        return total + jnp.dot(
            w_all[:, pl.ds(at, 512)], normed[pl.ds(at, 512), :], preferred_element_type=f32)

    both = lax.fori_loop(0, width // 512, product, jnp.zeros((4 * pad, 128), f32))
    gate, up = both[:2 * pad], both[2 * pad:]
    hidden = (gate / (1.0 + jnp.exp(-gate)) * up).astype(bf)
    hidden = jnp.concatenate([hidden, jnp.zeros((128 - 2 * pad, 128), bf)], axis=0)

    def piece(core, xx, zz):
        at = pl.multiple_of(dp_of(zz, xx, core) * cols, 16)
        return jnp.dot(d_cols[pl.ds(at, cols), :], hidden, preferred_element_type=f32)

    c_copies = []
    for zz in far_first:
        for k in range(NX):
            down[k, zz] = piece(1 - c, k, zz).astype(bf)
        c_copies.append(remote(down.at[:, zz], dc_buf.at[:, zz], twin))
    x_copies = []
    for zz, c_copy in zip(far_first, c_copies):
        c_copy.wait()
        sent = []
        for k, peer in enumerate(x_peers):
            d_mine[peer, zz] = (piece(c, peer, zz) + dc_buf[peer, zz].astype(f32)).astype(bf)
            sent.append(remote(d_mine.at[peer, zz], dx_buf.at[k, zz], (dp_of(z, peer, c), tp)))
        x_copies.append(sent)
    copies = []
    for zi, zz, sent in zip(far_index, far_first, x_copies):
        final = piece(c, x, zz) + dc_buf[x, zz].astype(f32)
        finish(sent)
        final = final + sum(dx_buf[k, zz].astype(f32) for k in range(3))
        if zi > 0:
            dz_src[zi - 1] = final.astype(bf)
            copies.append(remote(dz_src.at[zi - 1], dz_buf.at[zi - 1], (dp_of(zz, x, c), tp)))
    finish(copies)
    for k in range(7):
        final = final + dz_buf[k].astype(f32)
    share = cols // 4
    empty = jnp.zeros((y_out.shape[1] - share, 128), f32)
    for k in range(4):
        y_out[k] = jnp.concatenate([final[k * share:(k + 1) * share], empty], axis=0)
    y_in[tp] = y_out[tp]
    finish([remote(y_out.at[peer], y_in.at[tp], (me, peer)) for peer in y_peers])
    for t in range(2):
        own = attended[t].astype(f32)
        base = own[:share]
        for k in range(1, 4):
            base = jnp.where(tp == k, own[k * share:(k + 1) * share], base)
        lay_ref[t] = (base + (y_in[t] + y_in[t + 2])[:share]).astype(bf)


def tail(h, st, wo, res, gain, g0, g1, u0, u1, d0, d1, collective_id):
    vmem = pl.BlockSpec(memory_space=pltpu.VMEM)
    h = h.reshape((NC, NX, NZ) + h.shape[1:])
    rows, vd = h.shape[3:]
    cols, width = wo.shape[0], g0.shape[1]
    bf, f32 = jnp.bfloat16, jnp.float32
    pad = -(-g0.shape[0] // 16) * 16
    share = cols // 4
    tall = -(-share // 8) * 8
    shapes = [
        ((NX, NZ, rows, vd), bf), ((2, 32, 128), f32), ((NX, NZ, rows, vd), bf), ((2, 32, 128), f32),
        ((3, NZ, rows, vd), bf), ((3, 2, NZ, 128), f32), ((NZ, rows, vd), bf), ((NZ, 8, 128), f32),
        ((7, rows, vd), bf), ((7, 8, 128), f32),
        ((NZ, NX, NC, rows, vd), bf), ((NDP * rows, vd), f32), ((4,) + res.shape, bf),
        ((NZ, NX, NC, cols, 128), bf), ((width, 128), bf), ((4 * pad, width), bf), ((width, 128), bf),
        ((NX, NZ, cols, 128), bf), ((NX, NZ, cols, 128), bf), ((NX, NZ, cols, 128), bf), ((3, NZ, cols, 128), bf),
        ((7, cols, 128), bf), ((7, cols, 128), bf), ((4, tall, 128), f32), ((4, tall, 128), f32),
    ]
    return pl.pallas_call(
        tail_kernel,
        out_shape=(
            jax.ShapeDtypeStruct(res.shape, bf),
            jax.ShapeDtypeStruct((2, share, 128), bf),
        ),
        in_specs=[vmem] * 11,
        out_specs=(vmem, vmem),
        scratch_shapes=[pltpu.VMEM(shape, kind) for shape, kind in shapes]
        + [pltpu.SemaphoreType.DMA((168,)), pltpu.SemaphoreType.DMA((168,))],
        compiler_params=pltpu.CompilerParams(
            collective_id=collective_id, has_side_effects=True, vmem_limit_bytes=40 * 1024 * 1024),
        name="tail",
    )(h, st, wo, res, gain, g0, g1, u0, u1, d0, d1)


def per_device(
    pool, pool_owner, pool_slot, req_len, query, new_kv, resid, w_uv, w_out, ffn_gain, w_gate, w_up, w_down,
):
    bf = jnp.bfloat16
    d = lax.axis_index("dp")
    steps, requests, heads, key = query.shape
    width = pool.shape[1]
    swap = [(0, 1), (1, 0), (2, 3), (3, 2)]
    gate_t, up_t = w_gate.T, w_up.T
    gate_o, up_o, down_o = (lax.ppermute(w, "tp", swap) for w in (gate_t, up_t, w_down))

    info = jnp.stack([req_len // width, req_len % width], axis=1).reshape(4).astype(bf)
    info = jnp.broadcast_to(jnp.pad(info, (0, 60))[None], (4 * heads, 64))
    rows = jnp.transpose(query, (1, 0, 2, 3)).reshape(4 * heads, key)
    q_all = gather_dp(jnp.concatenate([rows, info], axis=1), 1)

    codes = q_all[:, 0, key:key + 4].astype(jnp.int32)
    lengths = codes[:, 0::2] * width + codes[:, 1::2]
    member = pool_owner[:, None] == jnp.arange(NDP, dtype=jnp.int32)[None, :]
    own_len = jnp.sum(jnp.where(member[:, :, None], lengths[None], 0), axis=1)
    first_blocks = (own_len[:, 0] + width - 1) // width
    part = (pool_slot >= first_blocks).astype(jnp.int32)
    index = pool_slot - part * first_blocks
    limit = jnp.where(part == 1, own_len[:, 1], own_len[:, 0]) - index * width
    two = jnp.arange(2, dtype=jnp.int32)
    owner = jnp.concatenate([pool_owner, jnp.full((2,), 0, jnp.int32) + d])
    part = jnp.concatenate([part, two])
    lim0 = jnp.concatenate([limit, jnp.full((2,), 1, jnp.int32)])
    lim1 = jnp.concatenate([limit, jnp.full((2,), 2, jnp.int32)])
    slot = owner % 2 * 32 + owner // 2 % 4 * 8 + owner // 8
    new_t = jnp.pad(jnp.transpose(new_kv, (1, 2, 0)), ((0, 0), (0, 0), (0, width - steps)))
    head_part, stats = attend(owner, slot, part, lim0, lim1, q_all, jnp.swapaxes(pool, 1, 2), new_t, w_uv)

    cols = resid.shape[2]
    gain = jnp.pad(ffn_gain.reshape(NDP, cols), ((0, 0), (0, 128 - cols)))
    attended, layer = tail(
        head_part, stats, w_out.T, jnp.swapaxes(resid, 1, 2), gain, gate_t, gate_o, up_t, up_o, w_down, down_o, 2
    )
    return jnp.swapaxes(attended, 1, 2), jnp.swapaxes(layer, 1, 2)


def solution(mesh):
    in_specs = (
        P("dp", None, None),
        P("dp"),
        P("dp"),
        P("dp"),
        P(None, "dp", "tp", None),
        P(None, "dp", None),
        P(None, None, "dp"),
        P("tp", None, None),
        P("tp", "dp"),
        P(),
        P(None, ("dp", "tp")),
        P(None, ("dp", "tp")),
        P(("dp", "tp"), None),
    )
    out_specs = (P(None, None, "dp"), P(None, None, ("dp", "tp")))
    return jax.shard_map(
        per_device, mesh=mesh, in_specs=in_specs, out_specs=out_specs, check_vma=False
    )
```

```python
import functools
import jax
import jax.numpy as jnp
from jax import lax
from jax.experimental import pallas as pl
from jax.experimental.pallas import tpu as pltpu
from jax.sharding import PartitionSpec as P

NZ, NX, NC = 8, 4, 2
NDP = NZ * NX * NC
LOW = -3.0e38
BIG = 56 * 1024 * 1024


def place():
    d = lax.axis_index("dp")
    return lax.div(d, 8), lax.rem(lax.div(d, 2), 4), lax.rem(d, 2), lax.axis_index("tp")


def dp_of(z, x, c):
    return (z * NX + x) * NC + c


def greet(peers):
    barrier = pltpu.get_barrier_semaphore()
    for peer in peers:
        pl.semaphore_signal(barrier, inc=1, device_id=peer, device_id_type=pl.DeviceIdType.MESH)
    pl.semaphore_wait(barrier, len(peers))


def gather_kernel(x_ref, out_ref, send, recv, twin_recv, own_sem, *, cut):
    z, x, c, tp = place()
    z_off, x_off = (1, 7, 2, 6, 3, 5, 4), (1, 3, 2)
    z_peers = {k: (dp_of(lax.rem(z + k, NZ), x, c), tp) for k in z_off}
    x_peers = {k: (dp_of(z, lax.rem(x + k, NX), c), tp) for k in x_off}
    to_twin = (dp_of(z, x, 1 - c), tp)
    greet([z_peers[1], z_peers[7], x_peers[1], x_peers[3], to_twin])
    spans = (pl.ds(0, cut), pl.ds(cut, x_ref.shape[0] - cut))
    started = []

    def push(at_z, at_x, part, peer, own=False):
        copy = pltpu.make_async_remote_copy(
            src_ref=x_ref.at[spans[part]] if own else out_ref.at[at_z, at_x, c, spans[part]],
            dst_ref=out_ref.at[at_z, at_x, c, spans[part]],
            send_sem=send.at[len(started)],
            recv_sem=recv.at[part, at_z, at_x],
            device_id=peer,
            device_id_type=pl.DeviceIdType.MESH,
        )
        copy.start()
        started.append(copy)

    def twin_copy(at_z, part, core, number):
        return pltpu.make_async_remote_copy(
            src_ref=out_ref.at[at_z, :, core, spans[part]],
            dst_ref=out_ref.at[at_z, :, core, spans[part]],
            send_sem=send.at[number],
            recv_sem=twin_recv.at[part, at_z],
            device_id=to_twin,
            device_id_type=pl.DeviceIdType.MESH,
        )

    def handle(part, kz, kx):
        own = kz == 0 and kx == 0
        at_z, at_x = (z if kz == 0 else lax.rem(z + NZ - kz, NZ)), (x if kx == 0 else lax.rem(x + NX - kx, NX))
        if own:
            pass
        else:
            pltpu.make_async_remote_copy(
                src_ref=x_ref.at[spans[part]],
                dst_ref=out_ref.at[at_z, at_x, c, spans[part]],
                send_sem=send.at[0],
                recv_sem=recv.at[part, at_z, at_x],
                device_id=to_twin,
                device_id_type=pl.DeviceIdType.MESH,
            ).wait_recv()
        up = 4 if part == 0 or kx % 2 == 0 else 3
        right = 2 if kz % 2 == 0 else 1
        along_z = part == 1 or kx == 0
        along_x = part == 0 or kz == 0
        if along_z and 0 <= kz < up:
            push(at_z, at_x, part, z_peers[1], own)
        if along_z and up - 7 < kz <= 0:
            push(at_z, at_x, part, z_peers[7], own)
        if along_x and 0 <= kx < right:
            push(at_z, at_x, part, x_peers[1], own)
        if along_x and right - 3 < kx <= 0:
            push(at_z, at_x, part, x_peers[3], own)

    events = []
    for part in range(2):
        for a in range(NZ):
            for b in range(NX):
                kz = a if a <= (4 if part == 0 or b % 2 == 0 else 3) else a - NZ
                kx = b if b <= (2 if a % 2 == 0 else 1) else b - NX
                when = abs(kz) + abs(kx) + 0.01 * (abs(kx) if part == 0 else abs(kz))
                events.append((when, part, a, b, kz, kx))
    own_copy = pltpu.make_async_copy(x_ref, out_ref.at[z, x, c], own_sem)
    own_copy.start()
    seen = {}
    for _, part, a, b, kz, kx in sorted(events, key=lambda e: e[0]):
        handle(part, kz, kx)
        seen[part, a] = seen.get((part, a), 0) + 1
        if seen[part, a] == NX:
            if a == 0 and part == min(p for p, q in seen if q == 0 and seen[p, q] == NX) and seen.get((1 - part, 0), 0) < NX:
                own_copy.wait()
            copy = twin_copy(lax.rem(z + NZ - a, NZ), part, c, len(started))
            copy.start()
            started.append(copy)
    for part in range(2):
        for at_z in range(NZ):
            twin_copy(at_z, part, 1 - c, 0).wait_recv()
    for copy in started:
        copy.wait_send()


def gather_dp(shard, collective_id, space=None, cut=48):
    space = pl.ANY if space is None else space
    return pl.pallas_call(
        functools.partial(gather_kernel, cut=cut),
        out_shape=jax.ShapeDtypeStruct((NZ, NX, NC) + shard.shape, shard.dtype),
        in_specs=[pl.BlockSpec(memory_space=space)],
        out_specs=pl.BlockSpec(memory_space=space),
        scratch_shapes=[
            pltpu.SemaphoreType.DMA((88,)),
            pltpu.SemaphoreType.DMA((2, NZ, NX)),
            pltpu.SemaphoreType.DMA((2, NZ)),
            pltpu.SemaphoreType.DMA,
        ],
        compiler_params=pltpu.CompilerParams(
            collective_id=collective_id, has_side_effects=True, vmem_limit_bytes=36 * 1024 * 1024
        ),
        name="gather_dp",
    )(shard).reshape((NDP,) + shard.shape)


def attend_kernel(owner_ref, slot_ref, code_ref, q_ref, blk_ref, new_ref, wuv_ref,
                  out_ref, stat_ref, acc, top, tot, table, *, per_step, heads):
    step = pl.program_id(0)
    rows = 2 * heads
    lat = wuv_ref.shape[1]
    scale = (3 * 64) ** (-0.5)
    width = blk_ref.shape[2]

    @pl.when(step == 0)
    def _():
        def clear(i, _):
            at = pl.multiple_of(i * 128, 128)
            for k in range(lat // 128):
                acc[k, pl.ds(at, 128), :] = jnp.zeros((128, 128), jnp.float32)
            top[pl.ds(at, 128), :] = jnp.full((128, 128), LOW, jnp.float32)
            tot[pl.ds(at, 128), :] = jnp.zeros((128, 128), jnp.float32)
            return 0

        lax.fori_loop(0, acc.shape[1] // 128, clear, 0)

    lane = lax.broadcasted_iota(jnp.int32, (rows, width), 1)
    late = lax.broadcasted_iota(jnp.int32, (rows, width), 0) >= heads

    def facts(number):
        group, slot = owner_ref[number], slot_ref[number]
        len0 = code_ref[group, 0] * width + code_ref[group, 1]
        len1 = code_ref[group, 2] * width + code_ref[group, 3]
        first = lax.div(len0 + width - 1, width)
        part = (slot >= first).astype(jnp.int32)
        limit = jnp.where(part == 1, len1, len0) - (slot - part * first) * width
        return group, part, limit

    def look(group, part, limit, block):
        both = jnp.dot(q_ref[group, :, :block.shape[0]], block, preferred_element_type=jnp.float32)
        scores = jnp.where(part == 0, both[:rows], both[rows:]) * scale
        keep = lane < limit
        peak = jnp.max(jnp.where(keep, scores, LOW), axis=1, keepdims=True)
        weights = jnp.where(keep, jnp.exp(scores - peak), 0.0)
        mixed = lax.dot_general(
            weights.astype(jnp.bfloat16), block[:lat], (((1,), (1,)), ((), ())),
            preferred_element_type=jnp.float32,
        )
        return peak, jnp.sum(weights, axis=1, keepdims=True), mixed

    def merge(group, part, found):
        peak, total, mixed = found
        place_of = lax.rem(group, 2) * 32 + lax.rem(lax.div(group, 2), 4) * 8 + lax.div(group, 8)
        at = pl.multiple_of((place_of * 2 + part) * rows, 8)
        old = top[pl.ds(at, rows), :]
        now = jnp.maximum(old, peak)
        fade, gain = jnp.exp(old - now), jnp.exp(peak - now)
        top[pl.ds(at, rows), :] = now
        tot[pl.ds(at, rows), :] = tot[pl.ds(at, rows), :] * fade + total * gain
        for k in range(lat // 128):
            acc[k, pl.ds(at, rows), :] = (
                acc[k, pl.ds(at, rows), :] * fade + mixed[:, k * 128:(k + 1) * 128] * gain)

    known = [facts(step * per_step + k) for k in range(per_step)]
    found = [look(*known[k], blk_ref[k]) for k in range(per_step)]
    for k in range(per_step):
        merge(*known[k][:2], found[k])

    @pl.when(step == pl.num_programs(0) - 1)
    def _():
        group = lax.axis_index("dp")
        for k in range(2):
            merge(group, k, look(group, k, jnp.where(late, 2, 1), new_ref[k]))

        def head(h, _):
            every = pl.ds(h, acc.shape[1] // heads, stride=heads)
            latent = jnp.concatenate([acc[k, every, :] for k in range(lat // 128)], axis=1).astype(jnp.bfloat16)
            table[every, :] = jnp.dot(
                latent, wuv_ref[h], preferred_element_type=jnp.float32)
            return 0

        lax.fori_loop(0, heads, head, 0, unroll=4)
        out_ref[...] = table[...].astype(jnp.bfloat16).reshape(out_ref.shape)
        column = lax.broadcasted_iota(jnp.int32, (2 * rows, 128), 1)

        def gather(j, carry):
            at = pl.multiple_of(j * 2 * rows, 8)
            return (jnp.where(column == j, top[pl.ds(at, 2 * rows), :], carry[0]),
                    jnp.where(column == j, tot[pl.ds(at, 2 * rows), :], carry[1]))

        zero = jnp.zeros((2 * rows, 128), jnp.float32)
        tops, tots = lax.fori_loop(0, NDP, gather, (zero, zero), unroll=4)
        pad = jnp.zeros((128 - 2 * rows, 128), jnp.float32)
        stat_ref[0] = jnp.concatenate([tops, pad], axis=0).T[:NDP]
        stat_ref[1] = jnp.concatenate([tots, pad], axis=0).T[:NDP]


def attend(owner, slot, codes, q_all, pool_t, new_t, w_uv, per_step=8):
    blocks, key, width = pool_t.shape
    heads, lat, vd = w_uv.shape
    total = NDP * 4 * heads
    vmem = pl.BlockSpec(memory_space=pltpu.VMEM)
    return pl.pallas_call(
        functools.partial(attend_kernel, per_step=per_step, heads=heads),
        out_shape=(
            jax.ShapeDtypeStruct((NDP, 4 * heads, vd), jnp.bfloat16),
            jax.ShapeDtypeStruct((2, NDP, 128), jnp.float32),
        ),
        grid_spec=pltpu.PrefetchScalarGridSpec(
            num_scalar_prefetch=3,
            grid=(blocks // per_step,),
            in_specs=[
                vmem,
                pl.BlockSpec((per_step, key, width), lambda i, *_: (i, 0, 0)),
                vmem,
                vmem,
            ],
            out_specs=[vmem, vmem],
            scratch_shapes=[
                pltpu.VMEM((lat // 128, total, 128), jnp.float32),
                pltpu.VMEM((total, 128), jnp.float32),
                pltpu.VMEM((total, 128), jnp.float32),
                pltpu.VMEM((total, vd), jnp.float32),
            ],
        ),
        compiler_params=pltpu.CompilerParams(vmem_limit_bytes=36 * 1024 * 1024, dimension_semantics=("arbitrary",)),
        name="attend",
    )(owner, slot, codes, q_all, pool_t, new_t, w_uv)


def columns_of(rows):
    count = rows.shape[0]
    if count < 128:
        rows = jnp.concatenate([rows, jnp.zeros((128 - count, 128), jnp.float32)], axis=0)
    return rows.T


def tail_kernel(h_ref, st_ref, wo_ref, res_ref, gain_ref, g0_ref, g1_ref, u0_ref, u1_ref, d0_ref, d1_ref,
                att_ref, lay_ref,
                c_buf, c_st, mine, m_st, x_buf, x_st, z_src, z_st, z_buf, z_in,
                h_all, h_flat, y_buf, a_all, normed, w_all, d_cols, down, dc_buf, d_mine, dx_buf, dz_src, dz_buf,
                y_out, y_in, send, recv):
    f32, bf = jnp.float32, jnp.bfloat16
    z, x, c, tp = place()
    z_off, x_off, x_back = (1, 7, 2, 6, 3, 5, 4), (1, 3, 2), (3, 1, 2)
    z_peers = [lax.rem(z + k, NZ) for k in z_off]
    x_peers = [lax.rem(x + k, NX) for k in x_off]
    y_peers = [lax.rem(tp + k, 4) for k in x_off]
    me = dp_of(z, x, c)
    twin = (dp_of(z, x, 1 - c), tp)
    greet(
        [(dp_of(k, x, c), tp) for k in z_peers] + [(dp_of(z, k, c), tp) for k in x_peers]
        + [(me, k) for k in y_peers] + [twin]
    )
    used = []

    def remote(src, dst, peer):
        copy = pltpu.make_async_remote_copy(
            src_ref=src, dst_ref=dst, send_sem=send.at[len(used)], recv_sem=recv.at[len(used)],
            device_id=peer, device_id_type=pl.DeviceIdType.MESH,
        )
        used.append(copy)
        copy.start()
        return copy

    def finish(copies):
        for copy in copies:
            copy.wait()

    half = NDP // 2
    there = pl.multiple_of((1 - c) * half, half)
    here = pl.multiple_of(c * half, half)
    far_first = [lax.rem(z + k, NZ) for k in (4, 3, 5, 2, 6, 1, 7, 0)]
    far_index = (4, 3, 5, 2, 6, 1, 7, 0)
    stat_copy = remote(st_ref.at[:, pl.ds(there, half)], c_st, twin)
    c_copies = [remote(h_ref.at[1 - c, :, zz], c_buf.at[:, zz], twin) for zz in far_first]
    units = g0_ref.shape[0]
    pad = w_all.shape[0] // 4
    width = w_all.shape[1]

    def prepare_rows():
        for k, ref in enumerate((g0_ref, g1_ref, u0_ref, u1_ref)):
            w_all[k * pad:(k + 1) * pad, :] = jnp.concatenate(
                [ref[...], jnp.zeros((pad - units, width), bf)], axis=0)

    def prepare_columns(start, stop):
        for k in range(start, stop):
            block = jnp.concatenate(
                [d0_ref[:, k * 128:(k + 1) * 128].astype(f32), jnp.zeros((pad - units, 128), f32),
                 d1_ref[:, k * 128:(k + 1) * 128].astype(f32), jnp.zeros((128 - pad - units, 128), f32)], axis=0)
            d_cols[k * 128:(k + 1) * 128, :] = block.T.astype(bf)

    tiles = width // 128
    stat_copy.wait()

    def relative(full):
        full = pltpu.roll(full, lax.rem(half - x * NZ, half), 0)
        return jnp.concatenate(
            [pltpu.roll(full[k * NZ:(k + 1) * NZ], lax.rem(NZ - z, NZ), 0) for k in range(NX)], axis=0)

    def merge(stats):
        tops = stats[0][0]
        for s in stats[1:]:
            tops = jnp.maximum(tops, s[0])
        factors = [jnp.exp(s[0] - tops) for s in stats]
        total = sum(f * s[1] for f, s in zip(factors, stats))
        return tops, total, [columns_of(f) for f in factors]

    rows = h_ref.shape[3]
    tops, total, columns = merge([
        [relative(st_ref[k, pl.ds(here, half), :]) for k in range(2)],
        [relative(c_st[k]) for k in range(2)],
    ])
    m_st[0] = tops
    m_st[1] = total
    x_stats = [
        remote(m_st.at[:, pl.ds(shift * NZ, NZ)], x_st.at[k], (dp_of(z, peer, c), tp))
        for k, (shift, peer) in enumerate(zip(x_off, x_peers))
    ]
    x_all = [x] + x_peers
    x_copies = []
    for zi, zz, c_copy in zip(far_index, far_first, c_copies):
        c_copy.wait()
        sent = []
        for k, peer in enumerate(x_all):
            n = (0, *x_off)[k] * NZ + zi
            mine[peer, zz] = (
                h_ref[c, peer, zz].astype(f32) * columns[0][:rows, n:n + 1]
                + c_buf[peer, zz].astype(f32) * columns[1][:rows, n:n + 1]
            ).astype(bf)
            if k > 0:
                sent.append(remote(mine.at[peer, zz], x_buf.at[k - 1, zz], (dp_of(z, peer, c), tp)))
        x_copies.append(sent)
    finish(x_stats)
    tops, total, columns = merge([m_st[:, 0:NZ, :]] + [x_st[k] for k in range(3)])
    copies = []
    for zi, zz, sent in zip(far_index, far_first, x_copies):
        finish(sent)
        z_src[zz] = (
            mine[x, zz].astype(f32) * columns[0][:rows, zi:zi + 1]
            + sum(x_buf[k, zz].astype(f32) * columns[k + 1][:rows, zi:zi + 1] for k in range(3))
        ).astype(bf)
        z_st[zz, 0:1, :] = tops[zi:zi + 1]
        z_st[zz, 1:2, :] = total[zi:zi + 1]
        z_st[zz, 2:8, :] = jnp.zeros((6, 128), f32)
        if zi > 0:
            dst = (dp_of(zz, x, c), tp)
            copies.append(remote(z_st.at[zz], z_in.at[zi - 1], dst))
            copies.append(remote(z_src.at[zz], z_buf.at[zi - 1], dst))
    finish(copies)
    stats = [z_st[z]] + [z_in[k] for k in range(7)]
    tops = jnp.concatenate([s[0:1] for s in stats], axis=0)
    tots = jnp.concatenate([s[1:2] for s in stats], axis=0)
    factor = jnp.exp(tops - jnp.max(tops, axis=0, keepdims=True))
    columns = columns_of(factor / jnp.sum(factor * tots, axis=0, keepdims=True))
    final = z_src[z].astype(f32) * columns[:rows, 0:1]
    for k in range(7):
        final = final + z_buf[k].astype(f32) * columns[:rows, k + 1:k + 2]

    def gather(buf, early, late):
        def ahead(zz, peer):
            return remote(buf.at[zz, x, c], buf.at[zz, x, c], (dp_of(z, peer, c), tp))

        first = [remote(buf.at[z, x, c], buf.at[z, x, c], (dp_of(peer, x, c), tp)) for peer in z_peers]
        second = [[ahead(z, peer)] for peer in x_peers]
        early()
        for k, copy in enumerate(first):
            copy.wait_recv()
            for row, peer in zip(second, x_peers):
                row.append(ahead(lax.rem(z + NZ - z_off[k], NZ), peer))
        third = [remote(buf.at[:, x, c], buf.at[:, x, c], twin)]
        late()
        for k, row in enumerate(second):
            for copy in row:
                copy.wait_recv()
            at = lax.rem(x + x_back[k], NX)
            third.append(remote(buf.at[:, at, c], buf.at[:, at, c], twin))
        for copy in third:
            copy.wait_recv()
        for copy in first + sum(second, []) + third:
            copy.wait_send()

    h_all[z, x, c] = final.astype(bf)
    gather(h_all, prepare_rows, functools.partial(prepare_columns, 0, tiles // 4))
    everyone = [(i, j, k) for i in range(NZ) for j in range(NX) for k in range(NC)]
    for n, (i, j, k) in enumerate(everyone):
        h_flat[n * rows:(n + 1) * rows, :] = h_all[i, j, k].astype(f32)
    heads = rows // 4
    for t in range(2):
        value = jnp.zeros(att_ref.shape[1:], f32)
        for h in range(0, heads, 2):
            both = jnp.concatenate(
                [h_flat[pl.ds(t * heads + h + k, 128, stride=rows // 2), :].astype(bf) for k in range(2)], axis=1)
            value = value + lax.dot_general(
                wo_ref[:, h * 128:(h + 2) * 128], both, (((1,), (1,)), ((), ())), preferred_element_type=f32)
        y_buf[tp, t] = value.astype(bf)
    copies = [remote(y_buf.at[tp], y_buf.at[tp], (me, peer)) for peer in y_peers]
    prepare_columns(tiles // 4, tiles // 2)
    finish(copies)
    attended = []
    for t in range(2):
        value = res_ref[t].astype(f32) + sum(y_buf[k, t].astype(f32) for k in range(4))
        attended.append(value.astype(bf))
        att_ref[t] = attended[t]
    odd = lax.rem(tp, 2)
    a_all[z, x, c] = jnp.where(odd == 0, attended[0].astype(f32), attended[1].astype(f32)).astype(bf)
    gather(
        a_all, functools.partial(prepare_columns, tiles // 2, tiles * 3 // 4),
        functools.partial(prepare_columns, tiles * 3 // 4, tiles))

    cols = att_ref.shape[1]
    square = jnp.zeros((8, 128), f32)
    for i, j, k in everyone:
        part = a_all[i, j, k].astype(f32)
        square = square + jnp.sum((part * part).reshape(cols // 8, 8, 128), axis=0)
    inverse = lax.rsqrt(jnp.sum(square, axis=0, keepdims=True) / width + 1e-6)
    gains = columns_of(gain_ref[...])
    for n, (i, j, k) in enumerate(everyone):
        normed[n * cols:(n + 1) * cols, :] = (
            a_all[i, j, k].astype(f32) * inverse * gains[:cols, n:n + 1]).astype(bf)

    def product(i, total):
        at = pl.multiple_of(i * 512, 512)
        return total + jnp.dot(
            w_all[:, pl.ds(at, 512)], normed[pl.ds(at, 512), :], preferred_element_type=f32)

    both = lax.fori_loop(0, width // 512, product, jnp.zeros((4 * pad, 128), f32))
    gate, up = both[:2 * pad], both[2 * pad:]
    hidden = (gate / (1.0 + jnp.exp(-gate)) * up).astype(bf)
    hidden = jnp.concatenate([hidden, jnp.zeros((128 - 2 * pad, 128), bf)], axis=0)

    def piece(core, xx, zz):
        at = pl.multiple_of(dp_of(zz, xx, core) * cols, 16)
        return jnp.dot(d_cols[pl.ds(at, cols), :], hidden, preferred_element_type=f32)

    c_copies = []
    for zz in far_first:
        for k in range(NX):
            down[k, zz] = piece(1 - c, k, zz).astype(bf)
        c_copies.append(remote(down.at[:, zz], dc_buf.at[:, zz], twin))
    x_copies = []
    for zz, c_copy in zip(far_first, c_copies):
        c_copy.wait()
        sent = []
        for k, peer in enumerate(x_peers):
            d_mine[peer, zz] = (piece(c, peer, zz) + dc_buf[peer, zz].astype(f32)).astype(bf)
            sent.append(remote(d_mine.at[peer, zz], dx_buf.at[k, zz], (dp_of(z, peer, c), tp)))
        x_copies.append(sent)
    copies = []
    for zi, zz, sent in zip(far_index, far_first, x_copies):
        final = piece(c, x, zz) + dc_buf[x, zz].astype(f32)
        finish(sent)
        final = final + sum(dx_buf[k, zz].astype(f32) for k in range(3))
        if zi > 0:
            dz_src[zi - 1] = final.astype(bf)
            copies.append(remote(dz_src.at[zi - 1], dz_buf.at[zi - 1], (dp_of(zz, x, c), tp)))
    finish(copies)
    for k in range(7):
        final = final + dz_buf[k].astype(f32)
    share = cols // 4
    empty = jnp.zeros((y_out.shape[1] - share, 128), f32)
    for k in range(4):
        y_out[k] = jnp.concatenate([final[k * share:(k + 1) * share], empty], axis=0)
    y_in[tp] = y_out[tp]
    finish([remote(y_out.at[peer], y_in.at[tp], (me, peer)) for peer in y_peers])
    for t in range(2):
        own = attended[t].astype(f32)
        base = own[:share]
        for k in range(1, 4):
            base = jnp.where(tp == k, own[k * share:(k + 1) * share], base)
        lay_ref[t] = (base + (y_in[t] + y_in[t + 2])[:share]).astype(bf)


def tail(h, st, wo, res, gain, g0, g1, u0, u1, d0, d1, collective_id):
    vmem = pl.BlockSpec(memory_space=pltpu.VMEM)
    h = h.reshape((NC, NX, NZ) + h.shape[1:])
    rows, vd = h.shape[3:]
    cols, width = wo.shape[0], g0.shape[1]
    bf, f32 = jnp.bfloat16, jnp.float32
    pad = -(-g0.shape[0] // 16) * 16
    share = cols // 4
    tall = -(-share // 8) * 8
    shapes = [
        ((NX, NZ, rows, vd), bf), ((2, 32, 128), f32), ((NX, NZ, rows, vd), bf), ((2, 32, 128), f32),
        ((3, NZ, rows, vd), bf), ((3, 2, NZ, 128), f32), ((NZ, rows, vd), bf), ((NZ, 8, 128), f32),
        ((7, rows, vd), bf), ((7, 8, 128), f32),
        ((NZ, NX, NC, rows, vd), bf), ((NDP * rows, vd), f32), ((4,) + res.shape, bf),
        ((NZ, NX, NC, cols, 128), bf), ((width, 128), bf), ((4 * pad, width), bf), ((width, 128), bf),
        ((NX, NZ, cols, 128), bf), ((NX, NZ, cols, 128), bf), ((NX, NZ, cols, 128), bf), ((3, NZ, cols, 128), bf),
        ((7, cols, 128), bf), ((7, cols, 128), bf), ((4, tall, 128), f32), ((4, tall, 128), f32),
    ]
    return pl.pallas_call(
        tail_kernel,
        out_shape=(
            jax.ShapeDtypeStruct(res.shape, bf),
            jax.ShapeDtypeStruct((2, share, 128), bf),
        ),
        in_specs=[vmem] * 11,
        out_specs=(vmem, vmem),
        scratch_shapes=[pltpu.VMEM(shape, kind) for shape, kind in shapes]
        + [pltpu.SemaphoreType.DMA((168,)), pltpu.SemaphoreType.DMA((168,))],
        compiler_params=pltpu.CompilerParams(
            collective_id=collective_id, has_side_effects=True, vmem_limit_bytes=40 * 1024 * 1024),
        name="tail",
    )(h, st, wo, res, gain, g0, g1, u0, u1, d0, d1)


def per_device(
    pool, pool_owner, pool_slot, req_len, query, new_kv, resid, w_uv, w_out, ffn_gain, w_gate, w_up, w_down,
):
    bf = jnp.bfloat16
    steps, requests, heads, key = query.shape
    width = pool.shape[1]
    swap = [(0, 1), (1, 0), (2, 3), (3, 2)]
    gate_t, up_t = w_gate.T, w_up.T
    gate_o, up_o, down_o = (lax.ppermute(w, "tp", swap) for w in (gate_t, up_t, w_down))

    info = jnp.stack([req_len // width, req_len % width], axis=1).reshape(4).astype(bf)
    info = jnp.broadcast_to(jnp.pad(info, (0, 60))[None], (4 * heads, 64))
    rows = jnp.transpose(query, (1, 0, 2, 3)).reshape(4 * heads, key)
    q_all = gather_dp(jnp.concatenate([rows, info], axis=1), 1)

    codes = q_all[:, 0, key:key + 4].astype(jnp.int32)
    new_t = jnp.pad(jnp.transpose(new_kv, (1, 2, 0)), ((0, 0), (0, 0), (0, width - steps)))
    head_part, stats = attend(pool_owner, pool_slot, codes, q_all, jnp.swapaxes(pool, 1, 2), new_t, w_uv)

    cols = resid.shape[2]
    gain = jnp.pad(ffn_gain.reshape(NDP, cols), ((0, 0), (0, 128 - cols)))
    attended, layer = tail(
        head_part, stats, w_out.T, jnp.swapaxes(resid, 1, 2), gain, gate_t, gate_o, up_t, up_o, w_down, down_o, 2
    )
    return jnp.swapaxes(attended, 1, 2), jnp.swapaxes(layer, 1, 2)


def solution(mesh):
    in_specs = (
        P("dp", None, None),
        P("dp"),
        P("dp"),
        P("dp"),
        P(None, "dp", "tp", None),
        P(None, "dp", None),
        P(None, None, "dp"),
        P("tp", None, None),
        P("tp", "dp"),
        P(),
        P(None, ("dp", "tp")),
        P(None, ("dp", "tp")),
        P(("dp", "tp"), None),
    )
    out_specs = (P(None, None, "dp"), P(None, None, ("dp", "tp")))
    return jax.shard_map(
        per_device, mesh=mesh, in_specs=in_specs, out_specs=out_specs, check_vma=False
    )
```

```python
import functools
import jax
import jax.numpy as jnp
from jax import lax
from jax.experimental import pallas as pl
from jax.experimental.pallas import tpu as pltpu
from jax.sharding import PartitionSpec as P

NZ, NX, NC = 8, 4, 2
NDP = NZ * NX * NC
LOW = -3.0e38
BIG = 56 * 1024 * 1024


def place():
    d = lax.axis_index("dp")
    return lax.div(d, 8), lax.rem(lax.div(d, 2), 4), lax.rem(d, 2), lax.axis_index("tp")


def dp_of(z, x, c):
    return (z * NX + x) * NC + c


def greet(peers):
    barrier = pltpu.get_barrier_semaphore()
    for peer in peers:
        pl.semaphore_signal(barrier, inc=1, device_id=peer, device_id_type=pl.DeviceIdType.MESH)
    pl.semaphore_wait(barrier, len(peers))


def gather_kernel(x_ref, new_ref, gain_ref, out_ref, send, recv, twin_recv, own_sem, *, cut):
    z, x, c, tp = place()
    z_off, x_off = (1, 7, 2, 6, 3, 5, 4), (1, 3, 2)
    z_peers = {k: (dp_of(lax.rem(z + k, NZ), x, c), tp) for k in z_off}
    x_peers = {k: (dp_of(z, lax.rem(x + k, NX), c), tp) for k in x_off}
    to_twin = (dp_of(z, x, 1 - c), tp)
    greet([z_peers[1], z_peers[7], x_peers[1], x_peers[3], to_twin])
    spans = (pl.ds(0, cut), pl.ds(cut, x_ref.shape[0] - cut))
    started = []

    def push(at_z, at_x, part, peer, own=False):
        copy = pltpu.make_async_remote_copy(
            src_ref=x_ref.at[spans[part]] if own else out_ref.at[at_z, at_x, c, spans[part]],
            dst_ref=out_ref.at[at_z, at_x, c, spans[part]],
            send_sem=send.at[len(started)],
            recv_sem=recv.at[part, at_z, at_x],
            device_id=peer,
            device_id_type=pl.DeviceIdType.MESH,
        )
        copy.start()
        started.append(copy)

    def twin_copy(at_z, part, core, number):
        return pltpu.make_async_remote_copy(
            src_ref=out_ref.at[at_z, :, core, spans[part]],
            dst_ref=out_ref.at[at_z, :, core, spans[part]],
            send_sem=send.at[number],
            recv_sem=twin_recv.at[part, at_z],
            device_id=to_twin,
            device_id_type=pl.DeviceIdType.MESH,
        )

    def handle(part, kz, kx):
        own = kz == 0 and kx == 0
        at_z, at_x = (z if kz == 0 else lax.rem(z + NZ - kz, NZ)), (x if kx == 0 else lax.rem(x + NX - kx, NX))
        if own:
            pass
        else:
            pltpu.make_async_remote_copy(
                src_ref=x_ref.at[spans[part]],
                dst_ref=out_ref.at[at_z, at_x, c, spans[part]],
                send_sem=send.at[0],
                recv_sem=recv.at[part, at_z, at_x],
                device_id=to_twin,
                device_id_type=pl.DeviceIdType.MESH,
            ).wait_recv()
        up = 4 if part == 0 or kx % 2 == 0 else 3
        right = 2 if kz % 2 == 0 else 1
        along_z = part == 1 or kx == 0
        along_x = part == 0 or kz == 0
        if along_z and 0 <= kz < up:
            push(at_z, at_x, part, z_peers[1], own)
        if along_z and up - 7 < kz <= 0:
            push(at_z, at_x, part, z_peers[7], own)
        if along_x and 0 <= kx < right:
            push(at_z, at_x, part, x_peers[1], own)
        if along_x and right - 3 < kx <= 0:
            push(at_z, at_x, part, x_peers[3], own)

    events = []
    for part in range(2):
        for a in range(NZ):
            for b in range(NX):
                kz = a if a <= (4 if part == 0 or b % 2 == 0 else 3) else a - NZ
                kx = b if b <= (2 if a % 2 == 0 else 1) else b - NX
                when = abs(kz) + abs(kx) + 0.01 * (abs(kx) if part == 0 else abs(kz))
                events.append((when, part, a, b, kz, kx))
    own_copy = pltpu.make_async_copy(x_ref, out_ref.at[z, x, c], own_sem)
    own_copy.start()
    seen = {}
    for _, part, a, b, kz, kx in sorted(events, key=lambda e: e[0]):
        handle(part, kz, kx)
        seen[part, a] = seen.get((part, a), 0) + 1
        if seen[part, a] == NX:
            if a == 0 and part == min(p for p, q in seen if q == 0 and seen[p, q] == NX) and seen.get((1 - part, 0), 0) < NX:
                own_copy.wait()
            copy = twin_copy(lax.rem(z + NZ - a, NZ), part, c, len(started))
            copy.start()
            started.append(copy)
    for part in range(2):
        for at_z in range(NZ):
            twin_copy(at_z, part, 1 - c, 0).wait_recv()
    for copy in started:
        copy.wait_send()


def gather_dp(shard, new_t, gain, collective_id, space=None, cut=48):
    space = pl.ANY if space is None else space
    return pl.pallas_call(
        functools.partial(gather_kernel, cut=cut),
        out_shape=jax.ShapeDtypeStruct((NZ, NX, NC) + shard.shape, shard.dtype),
        in_specs=[pl.BlockSpec(memory_space=space)] * 3,
        out_specs=pl.BlockSpec(memory_space=space),
        scratch_shapes=[
            pltpu.SemaphoreType.DMA((88,)),
            pltpu.SemaphoreType.DMA((2, NZ, NX)),
            pltpu.SemaphoreType.DMA((2, NZ)),
            pltpu.SemaphoreType.DMA,
        ],
        compiler_params=pltpu.CompilerParams(
            collective_id=collective_id, has_side_effects=True, vmem_limit_bytes=36 * 1024 * 1024
        ),
        name="gather_dp",
    )(shard, new_t, gain).reshape((NDP,) + shard.shape)


def attend_kernel(owner_ref, slot_ref, q_ref, blk_ref, new_ref, wuv_ref,
                  out_ref, stat_ref, code_rows, code_ref, code_sem, acc, top, tot, table, *, per_step, heads):
    step = pl.program_id(0)
    rows = 2 * heads
    lat = wuv_ref.shape[1]
    scale = (3 * 64) ** (-0.5)
    width = blk_ref.shape[2]

    key = blk_ref.shape[1]
    base = key // 128 * 128

    @pl.when(step == 0)
    def _():
        found = q_ref[:, 0:16, base:base + 128].astype(jnp.float32)
        code_rows[...] = jnp.max(found, axis=1).astype(jnp.int32)
        copy = pltpu.make_async_copy(code_rows, code_ref, code_sem)
        copy.start()

        def clear(i, _):
            at = pl.multiple_of(i * 128, 128)
            for k in range(lat // 128):
                acc[k, pl.ds(at, 128), :] = jnp.zeros((128, 128), jnp.float32)
            top[pl.ds(at, 128), :] = jnp.full((128, 128), LOW, jnp.float32)
            tot[pl.ds(at, 128), :] = jnp.zeros((128, 128), jnp.float32)
            return 0

        lax.fori_loop(0, acc.shape[1] // 128, clear, 0)
        copy.wait()

    lane = lax.broadcasted_iota(jnp.int32, (rows, width), 1)
    late = lax.broadcasted_iota(jnp.int32, (rows, width), 0) >= heads

    def facts(number):
        group, slot = owner_ref[number], slot_ref[number]
        code = [code_ref[group, key - base + k] for k in range(4)]
        len0, len1 = code[0] * width + code[1], code[2] * width + code[3]
        first = lax.div(len0 + width - 1, width)
        part = (slot >= first).astype(jnp.int32)
        limit = jnp.where(part == 1, len1, len0) - (slot - part * first) * width
        return group, part, limit

    def look(group, part, limit, block):
        both = jnp.dot(q_ref[group, :, :block.shape[0]], block, preferred_element_type=jnp.float32)
        scores = jnp.where(part == 0, both[:rows], both[rows:]) * scale
        keep = lane < limit
        peak = jnp.max(jnp.where(keep, scores, LOW), axis=1, keepdims=True)
        weights = jnp.where(keep, jnp.exp(scores - peak), 0.0)
        mixed = lax.dot_general(
            weights.astype(jnp.bfloat16), block[:lat], (((1,), (1,)), ((), ())),
            preferred_element_type=jnp.float32,
        )
        return peak, jnp.sum(weights, axis=1, keepdims=True), mixed

    def merge(group, part, found):
        peak, total, mixed = found
        place_of = lax.rem(group, 2) * 32 + lax.rem(lax.div(group, 2), 4) * 8 + lax.div(group, 8)
        at = pl.multiple_of((place_of * 2 + part) * rows, 8)
        old = top[pl.ds(at, rows), :]
        now = jnp.maximum(old, peak)
        fade, gain = jnp.exp(old - now), jnp.exp(peak - now)
        top[pl.ds(at, rows), :] = now
        tot[pl.ds(at, rows), :] = tot[pl.ds(at, rows), :] * fade + total * gain
        for k in range(lat // 128):
            acc[k, pl.ds(at, rows), :] = (
                acc[k, pl.ds(at, rows), :] * fade + mixed[:, k * 128:(k + 1) * 128] * gain)

    known = [facts(step * per_step + k) for k in range(per_step)]
    found = [look(*known[k], blk_ref[k]) for k in range(per_step)]
    for k in range(per_step):
        merge(*known[k][:2], found[k])

    @pl.when(step == pl.num_programs(0) - 1)
    def _():
        group = lax.axis_index("dp")
        for k in range(2):
            merge(group, k, look(group, k, jnp.where(late, 2, 1), new_ref[k]))

        def head(h, _):
            every = pl.ds(h, acc.shape[1] // heads, stride=heads)
            latent = jnp.concatenate([acc[k, every, :] for k in range(lat // 128)], axis=1).astype(jnp.bfloat16)
            table[every, :] = jnp.dot(
                latent, wuv_ref[h], preferred_element_type=jnp.float32)
            return 0

        lax.fori_loop(0, heads, head, 0, unroll=4)
        out_ref[...] = table[...].astype(jnp.bfloat16).reshape(out_ref.shape)
        column = lax.broadcasted_iota(jnp.int32, (2 * rows, 128), 1)

        def gather(j, carry):
            at = pl.multiple_of(j * 2 * rows, 8)
            return (jnp.where(column == j, top[pl.ds(at, 2 * rows), :], carry[0]),
                    jnp.where(column == j, tot[pl.ds(at, 2 * rows), :], carry[1]))

        zero = jnp.zeros((2 * rows, 128), jnp.float32)
        tops, tots = lax.fori_loop(0, NDP, gather, (zero, zero), unroll=4)
        pad = jnp.zeros((128 - 2 * rows, 128), jnp.float32)
        stat_ref[0] = jnp.concatenate([tops, pad], axis=0).T[:NDP]
        stat_ref[1] = jnp.concatenate([tots, pad], axis=0).T[:NDP]


def attend(owner, slot, q_all, pool_t, new_t, w_uv, per_step=8):
    blocks, key, width = pool_t.shape
    heads, lat, vd = w_uv.shape
    total = NDP * 4 * heads
    vmem = pl.BlockSpec(memory_space=pltpu.VMEM)
    return pl.pallas_call(
        functools.partial(attend_kernel, per_step=per_step, heads=heads),
        out_shape=(
            jax.ShapeDtypeStruct((NDP, 4 * heads, vd), jnp.bfloat16),
            jax.ShapeDtypeStruct((2, NDP, 128), jnp.float32),
        ),
        grid_spec=pltpu.PrefetchScalarGridSpec(
            num_scalar_prefetch=2,
            grid=(blocks // per_step,),
            in_specs=[
                vmem,
                pl.BlockSpec((per_step, key, width), lambda i, *_: (i, 0, 0)),
                vmem,
                vmem,
            ],
            out_specs=[vmem, vmem],
            scratch_shapes=[
                pltpu.VMEM((NDP, 128), jnp.int32),
                pltpu.SMEM((NDP, 128), jnp.int32),
                pltpu.SemaphoreType.DMA,
                pltpu.VMEM((lat // 128, total, 128), jnp.float32),
                pltpu.VMEM((total, 128), jnp.float32),
                pltpu.VMEM((total, 128), jnp.float32),
                pltpu.VMEM((total, vd), jnp.float32),
            ],
        ),
        compiler_params=pltpu.CompilerParams(vmem_limit_bytes=36 * 1024 * 1024, dimension_semantics=("arbitrary",)),
        name="attend",
    )(owner, slot, q_all, pool_t, new_t, w_uv)


def columns_of(rows):
    count = rows.shape[0]
    if count < 128:
        rows = jnp.concatenate([rows, jnp.zeros((128 - count, 128), jnp.float32)], axis=0)
    return rows.T


def tail_kernel(h_ref, st_ref, wo_ref, res_ref, gain_ref, g0_ref, g1_ref, u0_ref, u1_ref, d0_ref, d1_ref,
                att_ref, lay_ref,
                c_buf, c_st, mine, m_st, x_buf, x_st, z_src, z_st, z_buf, z_in,
                h_all, h_flat, y_buf, a_all, normed, w_all, d_cols, down, dc_buf, d_mine, dx_buf, dz_src, dz_buf,
                y_out, y_in, send, recv):
    f32, bf = jnp.float32, jnp.bfloat16
    z, x, c, tp = place()
    z_off, x_off, x_back = (1, 7, 2, 6, 3, 5, 4), (1, 3, 2), (3, 1, 2)
    z_peers = [lax.rem(z + k, NZ) for k in z_off]
    x_peers = [lax.rem(x + k, NX) for k in x_off]
    y_peers = [lax.rem(tp + k, 4) for k in x_off]
    me = dp_of(z, x, c)
    twin = (dp_of(z, x, 1 - c), tp)
    greet(
        [(dp_of(k, x, c), tp) for k in z_peers] + [(dp_of(z, k, c), tp) for k in x_peers]
        + [(me, k) for k in y_peers] + [twin]
    )
    used = []

    def remote(src, dst, peer):
        copy = pltpu.make_async_remote_copy(
            src_ref=src, dst_ref=dst, send_sem=send.at[len(used)], recv_sem=recv.at[len(used)],
            device_id=peer, device_id_type=pl.DeviceIdType.MESH,
        )
        used.append(copy)
        copy.start()
        return copy

    def finish(copies):
        for copy in copies:
            copy.wait()

    half = NDP // 2
    there = pl.multiple_of((1 - c) * half, half)
    here = pl.multiple_of(c * half, half)
    far_first = [lax.rem(z + k, NZ) for k in (4, 3, 5, 2, 6, 1, 7, 0)]
    far_index = (4, 3, 5, 2, 6, 1, 7, 0)
    stat_copy = remote(st_ref.at[:, pl.ds(there, half)], c_st, twin)
    c_copies = [remote(h_ref.at[1 - c, :, zz], c_buf.at[:, zz], twin) for zz in far_first]
    units = g0_ref.shape[0]
    pad = w_all.shape[0] // 4
    width = w_all.shape[1]

    def prepare_rows():
        for k, ref in enumerate((g0_ref, g1_ref, u0_ref, u1_ref)):
            w_all[k * pad:(k + 1) * pad, :] = jnp.concatenate(
                [ref[...], jnp.zeros((pad - units, width), bf)], axis=0)

    def prepare_columns(start, stop):
        for k in range(start, stop):
            block = jnp.concatenate(
                [d0_ref[:, k * 128:(k + 1) * 128].astype(f32), jnp.zeros((pad - units, 128), f32),
                 d1_ref[:, k * 128:(k + 1) * 128].astype(f32), jnp.zeros((128 - pad - units, 128), f32)], axis=0)
            d_cols[k * 128:(k + 1) * 128, :] = block.T.astype(bf)

    tiles = width // 128
    stat_copy.wait()

    def relative(full):
        full = pltpu.roll(full, lax.rem(half - x * NZ, half), 0)
        return jnp.concatenate(
            [pltpu.roll(full[k * NZ:(k + 1) * NZ], lax.rem(NZ - z, NZ), 0) for k in range(NX)], axis=0)

    def merge(stats):
        tops = stats[0][0]
        for s in stats[1:]:
            tops = jnp.maximum(tops, s[0])
        factors = [jnp.exp(s[0] - tops) for s in stats]
        total = sum(f * s[1] for f, s in zip(factors, stats))
        return tops, total, [columns_of(f) for f in factors]

    rows = h_ref.shape[3]
    tops, total, columns = merge([
        [relative(st_ref[k, pl.ds(here, half), :]) for k in range(2)],
        [relative(c_st[k]) for k in range(2)],
    ])
    m_st[0] = tops
    m_st[1] = total
    x_stats = [
        remote(m_st.at[:, pl.ds(shift * NZ, NZ)], x_st.at[k], (dp_of(z, peer, c), tp))
        for k, (shift, peer) in enumerate(zip(x_off, x_peers))
    ]
    x_all = [x] + x_peers
    x_copies = []
    for zi, zz, c_copy in zip(far_index, far_first, c_copies):
        c_copy.wait()
        sent = []
        for k, peer in enumerate(x_all):
            n = (0, *x_off)[k] * NZ + zi
            mine[peer, zz] = (
                h_ref[c, peer, zz].astype(f32) * columns[0][:rows, n:n + 1]
                + c_buf[peer, zz].astype(f32) * columns[1][:rows, n:n + 1]
            ).astype(bf)
            if k > 0:
                sent.append(remote(mine.at[peer, zz], x_buf.at[k - 1, zz], (dp_of(z, peer, c), tp)))
        x_copies.append(sent)
    finish(x_stats)
    tops, total, columns = merge([m_st[:, 0:NZ, :]] + [x_st[k] for k in range(3)])
    copies = []
    for zi, zz, sent in zip(far_index, far_first, x_copies):
        finish(sent)
        z_src[zz] = (
            mine[x, zz].astype(f32) * columns[0][:rows, zi:zi + 1]
            + sum(x_buf[k, zz].astype(f32) * columns[k + 1][:rows, zi:zi + 1] for k in range(3))
        ).astype(bf)
        z_st[zz, 0:1, :] = tops[zi:zi + 1]
        z_st[zz, 1:2, :] = total[zi:zi + 1]
        z_st[zz, 2:8, :] = jnp.zeros((6, 128), f32)
        if zi > 0:
            dst = (dp_of(zz, x, c), tp)
            copies.append(remote(z_st.at[zz], z_in.at[zi - 1], dst))
            copies.append(remote(z_src.at[zz], z_buf.at[zi - 1], dst))
    finish(copies)
    stats = [z_st[z]] + [z_in[k] for k in range(7)]
    tops = jnp.concatenate([s[0:1] for s in stats], axis=0)
    tots = jnp.concatenate([s[1:2] for s in stats], axis=0)
    factor = jnp.exp(tops - jnp.max(tops, axis=0, keepdims=True))
    columns = columns_of(factor / jnp.sum(factor * tots, axis=0, keepdims=True))
    final = z_src[z].astype(f32) * columns[:rows, 0:1]
    for k in range(7):
        final = final + z_buf[k].astype(f32) * columns[:rows, k + 1:k + 2]

    def gather(buf, early, late):
        def ahead(zz, peer):
            return remote(buf.at[zz, x, c], buf.at[zz, x, c], (dp_of(z, peer, c), tp))

        first = [remote(buf.at[z, x, c], buf.at[z, x, c], (dp_of(peer, x, c), tp)) for peer in z_peers]
        second = [[ahead(z, peer)] for peer in x_peers]
        early()
        for k, copy in enumerate(first):
            copy.wait_recv()
            for row, peer in zip(second, x_peers):
                row.append(ahead(lax.rem(z + NZ - z_off[k], NZ), peer))
        third = [remote(buf.at[:, x, c], buf.at[:, x, c], twin)]
        late()
        for k, row in enumerate(second):
            for copy in row:
                copy.wait_recv()
            at = lax.rem(x + x_back[k], NX)
            third.append(remote(buf.at[:, at, c], buf.at[:, at, c], twin))
        for copy in third:
            copy.wait_recv()
        for copy in first + sum(second, []) + third:
            copy.wait_send()

    h_all[z, x, c] = final.astype(bf)
    gather(h_all, prepare_rows, functools.partial(prepare_columns, 0, tiles // 4))
    everyone = [(i, j, k) for i in range(NZ) for j in range(NX) for k in range(NC)]
    for n, (i, j, k) in enumerate(everyone):
        h_flat[n * rows:(n + 1) * rows, :] = h_all[i, j, k].astype(f32)
    heads = rows // 4
    for t in range(2):
        value = jnp.zeros(att_ref.shape[1:], f32)
        for h in range(0, heads, 2):
            both = jnp.concatenate(
                [h_flat[pl.ds(t * heads + h + k, 128, stride=rows // 2), :].astype(bf) for k in range(2)], axis=1)
            value = value + lax.dot_general(
                wo_ref[:, h * 128:(h + 2) * 128], both, (((1,), (1,)), ((), ())), preferred_element_type=f32)
        y_buf[tp, t] = value.astype(bf)
    copies = [remote(y_buf.at[tp], y_buf.at[tp], (me, peer)) for peer in y_peers]
    prepare_columns(tiles // 4, tiles // 2)
    finish(copies)
    attended = []
    for t in range(2):
        value = res_ref[t].astype(f32) + sum(y_buf[k, t].astype(f32) for k in range(4))
        attended.append(value.astype(bf))
        att_ref[t] = attended[t]
    odd = lax.rem(tp, 2)
    a_all[z, x, c] = jnp.where(odd == 0, attended[0].astype(f32), attended[1].astype(f32)).astype(bf)
    gather(
        a_all, functools.partial(prepare_columns, tiles // 2, tiles * 3 // 4),
        functools.partial(prepare_columns, tiles * 3 // 4, tiles))

    cols = att_ref.shape[1]
    square = jnp.zeros((8, 128), f32)
    for i, j, k in everyone:
        part = a_all[i, j, k].astype(f32)
        square = square + jnp.sum((part * part).reshape(cols // 8, 8, 128), axis=0)
    inverse = lax.rsqrt(jnp.sum(square, axis=0, keepdims=True) / width + 1e-6)
    gains = columns_of(gain_ref[...])
    for n, (i, j, k) in enumerate(everyone):
        normed[n * cols:(n + 1) * cols, :] = (
            a_all[i, j, k].astype(f32) * inverse * gains[:cols, n:n + 1]).astype(bf)

    def product(i, total):
        at = pl.multiple_of(i * 512, 512)
        return total + jnp.dot(
            w_all[:, pl.ds(at, 512)], normed[pl.ds(at, 512), :], preferred_element_type=f32)

    both = lax.fori_loop(0, width // 512, product, jnp.zeros((4 * pad, 128), f32))
    gate, up = both[:2 * pad], both[2 * pad:]
    hidden = (gate / (1.0 + jnp.exp(-gate)) * up).astype(bf)
    hidden = jnp.concatenate([hidden, jnp.zeros((128 - 2 * pad, 128), bf)], axis=0)

    def piece(core, xx, zz):
        at = pl.multiple_of(dp_of(zz, xx, core) * cols, 16)
        return jnp.dot(d_cols[pl.ds(at, cols), :], hidden, preferred_element_type=f32)

    c_copies = []
    for zz in far_first:
        for k in range(NX):
            down[k, zz] = piece(1 - c, k, zz).astype(bf)
        c_copies.append(remote(down.at[:, zz], dc_buf.at[:, zz], twin))
    x_copies = []
    for zz, c_copy in zip(far_first, c_copies):
        c_copy.wait()
        sent = []
        for k, peer in enumerate(x_peers):
            d_mine[peer, zz] = (piece(c, peer, zz) + dc_buf[peer, zz].astype(f32)).astype(bf)
            sent.append(remote(d_mine.at[peer, zz], dx_buf.at[k, zz], (dp_of(z, peer, c), tp)))
        x_copies.append(sent)
    copies = []
    for zi, zz, sent in zip(far_index, far_first, x_copies):
        final = piece(c, x, zz) + dc_buf[x, zz].astype(f32)
        finish(sent)
        final = final + sum(dx_buf[k, zz].astype(f32) for k in range(3))
        if zi > 0:
            dz_src[zi - 1] = final.astype(bf)
            copies.append(remote(dz_src.at[zi - 1], dz_buf.at[zi - 1], (dp_of(zz, x, c), tp)))
    finish(copies)
    for k in range(7):
        final = final + dz_buf[k].astype(f32)
    share = cols // 4
    empty = jnp.zeros((y_out.shape[1] - share, 128), f32)
    for k in range(4):
        y_out[k] = jnp.concatenate([final[k * share:(k + 1) * share], empty], axis=0)
    y_in[tp] = y_out[tp]
    finish([remote(y_out.at[peer], y_in.at[tp], (me, peer)) for peer in y_peers])
    for t in range(2):
        own = attended[t].astype(f32)
        base = own[:share]
        for k in range(1, 4):
            base = jnp.where(tp == k, own[k * share:(k + 1) * share], base)
        lay_ref[t] = (base + (y_in[t] + y_in[t + 2])[:share]).astype(bf)


def tail(h, st, wo, res, gain, g0, g1, u0, u1, d0, d1, collective_id):
    vmem = pl.BlockSpec(memory_space=pltpu.VMEM)
    h = h.reshape((NC, NX, NZ) + h.shape[1:])
    rows, vd = h.shape[3:]
    cols, width = wo.shape[0], g0.shape[1]
    bf, f32 = jnp.bfloat16, jnp.float32
    pad = -(-g0.shape[0] // 16) * 16
    share = cols // 4
    tall = -(-share // 8) * 8
    shapes = [
        ((NX, NZ, rows, vd), bf), ((2, 32, 128), f32), ((NX, NZ, rows, vd), bf), ((2, 32, 128), f32),
        ((3, NZ, rows, vd), bf), ((3, 2, NZ, 128), f32), ((NZ, rows, vd), bf), ((NZ, 8, 128), f32),
        ((7, rows, vd), bf), ((7, 8, 128), f32),
        ((NZ, NX, NC, rows, vd), bf), ((NDP * rows, vd), f32), ((4,) + res.shape, bf),
        ((NZ, NX, NC, cols, 128), bf), ((width, 128), bf), ((4 * pad, width), bf), ((width, 128), bf),
        ((NX, NZ, cols, 128), bf), ((NX, NZ, cols, 128), bf), ((NX, NZ, cols, 128), bf), ((3, NZ, cols, 128), bf),
        ((7, cols, 128), bf), ((7, cols, 128), bf), ((4, tall, 128), f32), ((4, tall, 128), f32),
    ]
    return pl.pallas_call(
        tail_kernel,
        out_shape=(
            jax.ShapeDtypeStruct(res.shape, bf),
            jax.ShapeDtypeStruct((2, share, 128), bf),
        ),
        in_specs=[vmem] * 11,
        out_specs=(vmem, vmem),
        scratch_shapes=[pltpu.VMEM(shape, kind) for shape, kind in shapes]
        + [pltpu.SemaphoreType.DMA((168,)), pltpu.SemaphoreType.DMA((168,))],
        compiler_params=pltpu.CompilerParams(
            collective_id=collective_id, has_side_effects=True, vmem_limit_bytes=40 * 1024 * 1024),
        name="tail",
    )(h, st, wo, res, gain, g0, g1, u0, u1, d0, d1)


def per_device(
    pool, pool_owner, pool_slot, req_len, query, new_kv, resid, w_uv, w_out, ffn_gain, w_gate, w_up, w_down,
):
    bf = jnp.bfloat16
    steps, requests, heads, key = query.shape
    width = pool.shape[1]
    swap = [(0, 1), (1, 0), (2, 3), (3, 2)]
    gate_t, up_t = w_gate.T, w_up.T
    gate_o, up_o, down_o = (lax.ppermute(w, "tp", swap) for w in (gate_t, up_t, w_down))

    info = jnp.stack([req_len // width, req_len % width], axis=1).reshape(4).astype(bf)
    info = jnp.broadcast_to(jnp.pad(info, (0, 60))[None], (4 * heads, 64))
    rows = jnp.transpose(query, (1, 0, 2, 3)).reshape(4 * heads, key)
    new_t = jnp.pad(jnp.transpose(new_kv, (1, 2, 0)), ((0, 0), (0, 0), (0, width - steps)))
    cols = resid.shape[2]
    gain = jnp.pad(ffn_gain.reshape(NDP, cols), ((0, 0), (0, 128 - cols)))
    q_all = gather_dp(jnp.concatenate([rows, info], axis=1), new_t, gain, 1)
    head_part, stats = attend(pool_owner, pool_slot, q_all, jnp.swapaxes(pool, 1, 2), new_t, w_uv)

    attended, layer = tail(
        head_part, stats, w_out.T, jnp.swapaxes(resid, 1, 2), gain, gate_t, gate_o, up_t, up_o, w_down, down_o, 2
    )
    return jnp.swapaxes(attended, 1, 2), jnp.swapaxes(layer, 1, 2)


def solution(mesh):
    in_specs = (
        P("dp", None, None),
        P("dp"),
        P("dp"),
        P("dp"),
        P(None, "dp", "tp", None),
        P(None, "dp", None),
        P(None, None, "dp"),
        P("tp", None, None),
        P("tp", "dp"),
        P(),
        P(None, ("dp", "tp")),
        P(None, ("dp", "tp")),
        P(("dp", "tp"), None),
    )
    out_specs = (P(None, None, "dp"), P(None, None, ("dp", "tp")))
    return jax.shard_map(
        per_device, mesh=mesh, in_specs=in_specs, out_specs=out_specs, check_vma=False
    )
```

```python
import functools
import jax
import jax.numpy as jnp
from jax import lax
from jax.experimental import pallas as pl
from jax.experimental.pallas import tpu as pltpu
from jax.sharding import PartitionSpec as P

NZ, NX, NC = 8, 4, 2
NDP = NZ * NX * NC
LOW = -3.0e38
BIG = 56 * 1024 * 1024


def place():
    d = lax.axis_index("dp")
    return lax.div(d, 8), lax.rem(lax.div(d, 2), 4), lax.rem(d, 2), lax.axis_index("tp")


def dp_of(z, x, c):
    return (z * NX + x) * NC + c


def greet(peers):
    barrier = pltpu.get_barrier_semaphore()
    for peer in peers:
        pl.semaphore_signal(barrier, inc=1, device_id=peer, device_id_type=pl.DeviceIdType.MESH)
    pl.semaphore_wait(barrier, len(peers))


def gather_kernel(x_ref, out_ref, send, recv, twin_recv, own_sem, *, cut):
    z, x, c, tp = place()
    z_off, x_off = (1, 7, 2, 6, 3, 5, 4), (1, 3, 2)
    z_peers = {k: (dp_of(lax.rem(z + k, NZ), x, c), tp) for k in z_off}
    x_peers = {k: (dp_of(z, lax.rem(x + k, NX), c), tp) for k in x_off}
    to_twin = (dp_of(z, x, 1 - c), tp)
    greet([z_peers[1], z_peers[7], x_peers[1], x_peers[3], to_twin])
    spans = (pl.ds(0, cut), pl.ds(cut, x_ref.shape[0] - cut))
    started = []

    def push(at_z, at_x, part, peer, own=False):
        copy = pltpu.make_async_remote_copy(
            src_ref=x_ref.at[spans[part]] if own else out_ref.at[at_z, at_x, c, spans[part]],
            dst_ref=out_ref.at[at_z, at_x, c, spans[part]],
            send_sem=send.at[len(started)],
            recv_sem=recv.at[part, at_z, at_x],
            device_id=peer,
            device_id_type=pl.DeviceIdType.MESH,
        )
        copy.start()
        started.append(copy)

    def twin_copy(at_z, part, core, number):
        return pltpu.make_async_remote_copy(
            src_ref=out_ref.at[at_z, :, core, spans[part]],
            dst_ref=out_ref.at[at_z, :, core, spans[part]],
            send_sem=send.at[number],
            recv_sem=twin_recv.at[part, at_z],
            device_id=to_twin,
            device_id_type=pl.DeviceIdType.MESH,
        )

    def handle(part, kz, kx):
        own = kz == 0 and kx == 0
        at_z, at_x = (z if kz == 0 else lax.rem(z + NZ - kz, NZ)), (x if kx == 0 else lax.rem(x + NX - kx, NX))
        if own:
            pass
        else:
            pltpu.make_async_remote_copy(
                src_ref=x_ref.at[spans[part]],
                dst_ref=out_ref.at[at_z, at_x, c, spans[part]],
                send_sem=send.at[0],
                recv_sem=recv.at[part, at_z, at_x],
                device_id=to_twin,
                device_id_type=pl.DeviceIdType.MESH,
            ).wait_recv()
        up = 4 if part == 0 or kx % 2 == 0 else 3
        right = 2 if kz % 2 == 0 else 1
        along_z = part == 1 or kx == 0
        along_x = part == 0 or kz == 0
        if along_z and 0 <= kz < up:
            push(at_z, at_x, part, z_peers[1], own)
        if along_z and up - 7 < kz <= 0:
            push(at_z, at_x, part, z_peers[7], own)
        if along_x and 0 <= kx < right:
            push(at_z, at_x, part, x_peers[1], own)
        if along_x and right - 3 < kx <= 0:
            push(at_z, at_x, part, x_peers[3], own)

    events = []
    for part in range(2):
        for a in range(NZ):
            for b in range(NX):
                kz = a if a <= (4 if part == 0 or b % 2 == 0 else 3) else a - NZ
                kx = b if b <= (2 if a % 2 == 0 else 1) else b - NX
                when = abs(kz) + abs(kx) + 0.01 * (abs(kx) if part == 0 else abs(kz))
                events.append((when, part, a, b, kz, kx))
    own_copy = pltpu.make_async_copy(x_ref, out_ref.at[z, x, c], own_sem)
    own_copy.start()
    seen = {}
    for _, part, a, b, kz, kx in sorted(events, key=lambda e: e[0]):
        handle(part, kz, kx)
        seen[part, a] = seen.get((part, a), 0) + 1
        if seen[part, a] == NX:
            if a == 0 and part == min(p for p, q in seen if q == 0 and seen[p, q] == NX) and seen.get((1 - part, 0), 0) < NX:
                own_copy.wait()
            copy = twin_copy(lax.rem(z + NZ - a, NZ), part, c, len(started))
            copy.start()
            started.append(copy)
    for part in range(2):
        for at_z in range(NZ):
            twin_copy(at_z, part, 1 - c, 0).wait_recv()
    for copy in started:
        copy.wait_send()


def gather_dp(shard, collective_id, space=None, cut=48):
    space = pl.ANY if space is None else space
    return pl.pallas_call(
        functools.partial(gather_kernel, cut=cut),
        out_shape=jax.ShapeDtypeStruct((NZ, NX, NC) + shard.shape, shard.dtype),
        in_specs=[pl.BlockSpec(memory_space=space)],
        out_specs=pl.BlockSpec(memory_space=space),
        scratch_shapes=[
            pltpu.SemaphoreType.DMA((88,)),
            pltpu.SemaphoreType.DMA((2, NZ, NX)),
            pltpu.SemaphoreType.DMA((2, NZ)),
            pltpu.SemaphoreType.DMA,
        ],
        compiler_params=pltpu.CompilerParams(
            collective_id=collective_id, has_side_effects=True, vmem_limit_bytes=36 * 1024 * 1024
        ),
        name="gather_dp",
    )(shard).reshape((NDP,) + shard.shape)


def attend_kernel(owner_ref, slot_ref, q_ref, blk_ref, new_ref, wuv_ref,
                  out_ref, stat_ref, code_rows, code_ref, code_sem, acc, top, tot, table, *, per_step, heads):
    step = pl.program_id(0)
    rows = 2 * heads
    lat = wuv_ref.shape[1]
    scale = (3 * 64) ** (-0.5)
    width = blk_ref.shape[2]

    key = blk_ref.shape[1]
    base = key // 128 * 128

    @pl.when(step == 0)
    def _():
        found = q_ref[:, 0:16, base:base + 128].astype(jnp.float32)
        code_rows[...] = jnp.max(found, axis=1).astype(jnp.int32)
        copy = pltpu.make_async_copy(code_rows, code_ref, code_sem)
        copy.start()

        def clear(i, _):
            at = pl.multiple_of(i * 128, 128)
            for k in range(lat // 128):
                acc[k, pl.ds(at, 128), :] = jnp.zeros((128, 128), jnp.float32)
            top[pl.ds(at, 128), :] = jnp.full((128, 128), LOW, jnp.float32)
            tot[pl.ds(at, 128), :] = jnp.zeros((128, 128), jnp.float32)
            return 0

        lax.fori_loop(0, acc.shape[1] // 128, clear, 0)
        copy.wait()

    lane = lax.broadcasted_iota(jnp.int32, (rows, width), 1)
    late = lax.broadcasted_iota(jnp.int32, (rows, width), 0) >= heads

    def facts(number):
        group, slot = owner_ref[number], slot_ref[number]
        code = [code_ref[group, key - base + k] for k in range(4)]
        len0, len1 = code[0] * width + code[1], code[2] * width + code[3]
        first = lax.div(len0 + width - 1, width)
        part = (slot >= first).astype(jnp.int32)
        limit = jnp.where(part == 1, len1, len0) - (slot - part * first) * width
        return group, part, limit

    def look(group, part, limit, block, natural=False):
        both = lax.dot_general(
            q_ref[group, :, :key], block, (((1,), (1 if natural else 0,)), ((), ())),
            preferred_element_type=jnp.float32,
        )
        scores = jnp.where(part == 0, both[:rows], both[rows:]) * scale
        keep = lane < limit
        peak = jnp.max(jnp.where(keep, scores, LOW), axis=1, keepdims=True)
        weights = jnp.where(keep, jnp.exp(scores - peak), 0.0)
        mixed = lax.dot_general(
            weights.astype(jnp.bfloat16), block[:, :lat] if natural else block[:lat],
            (((1,), (0 if natural else 1,)), ((), ())),
            preferred_element_type=jnp.float32,
        )
        return peak, jnp.sum(weights, axis=1, keepdims=True), mixed

    def merge(group, part, found):
        peak, total, mixed = found
        place_of = lax.rem(group, 2) * 32 + lax.rem(lax.div(group, 2), 4) * 8 + lax.div(group, 8)
        at = pl.multiple_of((place_of * 2 + part) * rows, 8)
        old = top[pl.ds(at, rows), :]
        now = jnp.maximum(old, peak)
        fade, gain = jnp.exp(old - now), jnp.exp(peak - now)
        top[pl.ds(at, rows), :] = now
        tot[pl.ds(at, rows), :] = tot[pl.ds(at, rows), :] * fade + total * gain
        for k in range(lat // 128):
            acc[k, pl.ds(at, rows), :] = (
                acc[k, pl.ds(at, rows), :] * fade + mixed[:, k * 128:(k + 1) * 128] * gain)

    known = [facts(step * per_step + k) for k in range(per_step)]
    found = [look(*known[k], blk_ref[k]) for k in range(per_step)]
    for k in range(per_step):
        merge(*known[k][:2], found[k])

    @pl.when(step == pl.num_programs(0) - 1)
    def _():
        group = lax.axis_index("dp")
        for k in range(2):
            which = lax.broadcasted_iota(jnp.int32, (width, key), 0)
            first, second = (new_ref[u].astype(jnp.float32)[k:k + 1] for u in range(2))
            block = jnp.where(which == 0, first, jnp.where(which == 1, second, 0.0)).astype(jnp.bfloat16)
            merge(group, k, look(group, k, jnp.where(late, 2, 1), block, True))

        def head(h, _):
            every = pl.ds(h, acc.shape[1] // heads, stride=heads)
            latent = jnp.concatenate([acc[k, every, :] for k in range(lat // 128)], axis=1).astype(jnp.bfloat16)
            table[every, :] = jnp.dot(
                latent, wuv_ref[h], preferred_element_type=jnp.float32)
            return 0

        lax.fori_loop(0, heads, head, 0, unroll=4)
        out_ref[...] = table[...].astype(jnp.bfloat16).reshape(out_ref.shape)
        column = lax.broadcasted_iota(jnp.int32, (2 * rows, 128), 1)

        def gather(j, carry):
            at = pl.multiple_of(j * 2 * rows, 8)
            return (jnp.where(column == j, top[pl.ds(at, 2 * rows), :], carry[0]),
                    jnp.where(column == j, tot[pl.ds(at, 2 * rows), :], carry[1]))

        zero = jnp.zeros((2 * rows, 128), jnp.float32)
        tops, tots = lax.fori_loop(0, NDP, gather, (zero, zero), unroll=4)
        pad = jnp.zeros((128 - 2 * rows, 128), jnp.float32)
        stat_ref[0] = jnp.concatenate([tops, pad], axis=0).T[:NDP]
        stat_ref[1] = jnp.concatenate([tots, pad], axis=0).T[:NDP]


def attend(owner, slot, q_all, pool_t, new_t, w_uv, per_step=8):
    blocks, key, width = pool_t.shape
    heads, lat, vd = w_uv.shape
    total = NDP * 4 * heads
    vmem = pl.BlockSpec(memory_space=pltpu.VMEM)
    return pl.pallas_call(
        functools.partial(attend_kernel, per_step=per_step, heads=heads),
        out_shape=(
            jax.ShapeDtypeStruct((NDP, 4 * heads, vd), jnp.bfloat16),
            jax.ShapeDtypeStruct((2, NDP, 128), jnp.float32),
        ),
        grid_spec=pltpu.PrefetchScalarGridSpec(
            num_scalar_prefetch=2,
            grid=(blocks // per_step,),
            in_specs=[
                vmem,
                pl.BlockSpec((per_step, key, width), lambda i, *_: (i, 0, 0)),
                vmem,
                vmem,
            ],
            out_specs=[vmem, vmem],
            scratch_shapes=[
                pltpu.VMEM((NDP, 128), jnp.int32),
                pltpu.SMEM((NDP, 128), jnp.int32),
                pltpu.SemaphoreType.DMA,
                pltpu.VMEM((lat // 128, total, 128), jnp.float32),
                pltpu.VMEM((total, 128), jnp.float32),
                pltpu.VMEM((total, 128), jnp.float32),
                pltpu.VMEM((total, vd), jnp.float32),
            ],
        ),
        compiler_params=pltpu.CompilerParams(vmem_limit_bytes=36 * 1024 * 1024, dimension_semantics=("arbitrary",)),
        name="attend",
    )(owner, slot, q_all, pool_t, new_t, w_uv)


def columns_of(rows):
    count = rows.shape[0]
    if count < 128:
        rows = jnp.concatenate([rows, jnp.zeros((128 - count, 128), jnp.float32)], axis=0)
    return rows.T


def tail_kernel(h_ref, st_ref, wo_ref, res_ref, gain_ref, g0_ref, g1_ref, u0_ref, u1_ref, d0_ref, d1_ref,
                att_ref, lay_ref,
                c_buf, c_st, mine, m_st, x_buf, x_st, z_src, z_st, z_buf, z_in,
                h_all, h_flat, y_buf, a_all, normed, w_all, d_cols, down, dc_buf, d_mine, dx_buf, dz_src, dz_buf,
                y_out, y_in, send, recv):
    f32, bf = jnp.float32, jnp.bfloat16
    z, x, c, tp = place()
    z_off, x_off, x_back = (1, 7, 2, 6, 3, 5, 4), (1, 3, 2), (3, 1, 2)
    z_peers = [lax.rem(z + k, NZ) for k in z_off]
    x_peers = [lax.rem(x + k, NX) for k in x_off]
    y_peers = [lax.rem(tp + k, 4) for k in x_off]
    me = dp_of(z, x, c)
    twin = (dp_of(z, x, 1 - c), tp)
    greet(
        [(dp_of(k, x, c), tp) for k in z_peers] + [(dp_of(z, k, c), tp) for k in x_peers]
        + [(me, k) for k in y_peers] + [twin]
    )
    used = []

    def remote(src, dst, peer):
        copy = pltpu.make_async_remote_copy(
            src_ref=src, dst_ref=dst, send_sem=send.at[len(used)], recv_sem=recv.at[len(used)],
            device_id=peer, device_id_type=pl.DeviceIdType.MESH,
        )
        used.append(copy)
        copy.start()
        return copy

    def finish(copies):
        for copy in copies:
            copy.wait()

    half = NDP // 2
    there = pl.multiple_of((1 - c) * half, half)
    here = pl.multiple_of(c * half, half)
    far_first = [lax.rem(z + k, NZ) for k in (4, 3, 5, 2, 6, 1, 7, 0)]
    far_index = (4, 3, 5, 2, 6, 1, 7, 0)
    stat_copy = remote(st_ref.at[:, pl.ds(there, half)], c_st, twin)
    c_copies = [remote(h_ref.at[1 - c, :, zz], c_buf.at[:, zz], twin) for zz in far_first]
    units = g0_ref.shape[0]
    pad = w_all.shape[0] // 4
    width = w_all.shape[1]

    def prepare_rows():
        for k, ref in enumerate((g0_ref, g1_ref, u0_ref, u1_ref)):
            w_all[k * pad:(k + 1) * pad, :] = jnp.concatenate(
                [ref[...], jnp.zeros((pad - units, width), bf)], axis=0)

    def prepare_columns(start, stop):
        for k in range(start, stop):
            block = jnp.concatenate(
                [d0_ref[:, k * 128:(k + 1) * 128].astype(f32), jnp.zeros((pad - units, 128), f32),
                 d1_ref[:, k * 128:(k + 1) * 128].astype(f32), jnp.zeros((128 - pad - units, 128), f32)], axis=0)
            d_cols[k * 128:(k + 1) * 128, :] = block.T.astype(bf)

    tiles = width // 128
    stat_copy.wait()

    def relative(full):
        full = pltpu.roll(full, lax.rem(half - x * NZ, half), 0)
        return jnp.concatenate(
            [pltpu.roll(full[k * NZ:(k + 1) * NZ], lax.rem(NZ - z, NZ), 0) for k in range(NX)], axis=0)

    def merge(stats):
        tops = stats[0][0]
        for s in stats[1:]:
            tops = jnp.maximum(tops, s[0])
        factors = [jnp.exp(s[0] - tops) for s in stats]
        total = sum(f * s[1] for f, s in zip(factors, stats))
        return tops, total, [columns_of(f) for f in factors]

    rows = h_ref.shape[3]
    tops, total, columns = merge([
        [relative(st_ref[k, pl.ds(here, half), :]) for k in range(2)],
        [relative(c_st[k]) for k in range(2)],
    ])
    m_st[0] = tops
    m_st[1] = total
    x_stats = [
        remote(m_st.at[:, pl.ds(shift * NZ, NZ)], x_st.at[k], (dp_of(z, peer, c), tp))
        for k, (shift, peer) in enumerate(zip(x_off, x_peers))
    ]
    x_all = [x] + x_peers
    x_copies = []
    for zi, zz, c_copy in zip(far_index, far_first, c_copies):
        c_copy.wait()
        sent = []
        for k, peer in enumerate(x_all):
            n = (0, *x_off)[k] * NZ + zi
            mine[peer, zz] = (
                h_ref[c, peer, zz].astype(f32) * columns[0][:rows, n:n + 1]
                + c_buf[peer, zz].astype(f32) * columns[1][:rows, n:n + 1]
            ).astype(bf)
            if k > 0:
                sent.append(remote(mine.at[peer, zz], x_buf.at[k - 1, zz], (dp_of(z, peer, c), tp)))
        x_copies.append(sent)
    finish(x_stats)
    tops, total, columns = merge([m_st[:, 0:NZ, :]] + [x_st[k] for k in range(3)])
    copies = []
    for zi, zz, sent in zip(far_index, far_first, x_copies):
        finish(sent)
        z_src[zz] = (
            mine[x, zz].astype(f32) * columns[0][:rows, zi:zi + 1]
            + sum(x_buf[k, zz].astype(f32) * columns[k + 1][:rows, zi:zi + 1] for k in range(3))
        ).astype(bf)
        z_st[zz, 0:1, :] = tops[zi:zi + 1]
        z_st[zz, 1:2, :] = total[zi:zi + 1]
        z_st[zz, 2:8, :] = jnp.zeros((6, 128), f32)
        if zi > 0:
            dst = (dp_of(zz, x, c), tp)
            copies.append(remote(z_st.at[zz], z_in.at[zi - 1], dst))
            copies.append(remote(z_src.at[zz], z_buf.at[zi - 1], dst))
    finish(copies)
    stats = [z_st[z]] + [z_in[k] for k in range(7)]
    tops = jnp.concatenate([s[0:1] for s in stats], axis=0)
    tots = jnp.concatenate([s[1:2] for s in stats], axis=0)
    factor = jnp.exp(tops - jnp.max(tops, axis=0, keepdims=True))
    columns = columns_of(factor / jnp.sum(factor * tots, axis=0, keepdims=True))
    final = z_src[z].astype(f32) * columns[:rows, 0:1]
    for k in range(7):
        final = final + z_buf[k].astype(f32) * columns[:rows, k + 1:k + 2]

    def gather(buf, early, late):
        def ahead(zz, peer):
            return remote(buf.at[zz, x, c], buf.at[zz, x, c], (dp_of(z, peer, c), tp))

        first = [remote(buf.at[z, x, c], buf.at[z, x, c], (dp_of(peer, x, c), tp)) for peer in z_peers]
        second = [[ahead(z, peer)] for peer in x_peers]
        early()
        for k, copy in enumerate(first):
            copy.wait_recv()
            for row, peer in zip(second, x_peers):
                row.append(ahead(lax.rem(z + NZ - z_off[k], NZ), peer))
        third = [remote(buf.at[:, x, c], buf.at[:, x, c], twin)]
        late()
        for k, row in enumerate(second):
            for copy in row:
                copy.wait_recv()
            at = lax.rem(x + x_back[k], NX)
            third.append(remote(buf.at[:, at, c], buf.at[:, at, c], twin))
        for copy in third:
            copy.wait_recv()
        for copy in first + sum(second, []) + third:
            copy.wait_send()

    h_all[z, x, c] = final.astype(bf)
    gather(h_all, prepare_rows, functools.partial(prepare_columns, 0, tiles // 4))
    everyone = [(i, j, k) for i in range(NZ) for j in range(NX) for k in range(NC)]
    for n, (i, j, k) in enumerate(everyone):
        h_flat[n * rows:(n + 1) * rows, :] = h_all[i, j, k].astype(f32)
    heads = rows // 4
    for t in range(2):
        value = jnp.zeros(att_ref.shape[1:], f32)
        for h in range(0, heads, 2):
            both = jnp.concatenate(
                [h_flat[pl.ds(t * heads + h + k, 128, stride=rows // 2), :].astype(bf) for k in range(2)], axis=1)
            value = value + lax.dot_general(
                wo_ref[:, h * 128:(h + 2) * 128], both, (((1,), (1,)), ((), ())), preferred_element_type=f32)
        y_buf[tp, t] = value.astype(bf)
    copies = [remote(y_buf.at[tp], y_buf.at[tp], (me, peer)) for peer in y_peers]
    prepare_columns(tiles // 4, tiles // 2)
    finish(copies)
    attended = []
    for t in range(2):
        value = res_ref[t].astype(f32) + sum(y_buf[k, t].astype(f32) for k in range(4))
        attended.append(value.astype(bf))
        att_ref[t] = attended[t]
    odd = lax.rem(tp, 2)
    a_all[z, x, c] = jnp.where(odd == 0, attended[0].astype(f32), attended[1].astype(f32)).astype(bf)
    gather(
        a_all, functools.partial(prepare_columns, tiles // 2, tiles * 3 // 4),
        functools.partial(prepare_columns, tiles * 3 // 4, tiles))

    cols = att_ref.shape[1]
    square = jnp.zeros((8, 128), f32)
    for i, j, k in everyone:
        part = a_all[i, j, k].astype(f32)
        square = square + jnp.sum((part * part).reshape(cols // 8, 8, 128), axis=0)
    inverse = lax.rsqrt(jnp.sum(square, axis=0, keepdims=True) / width + 1e-6)
    gains = columns_of(gain_ref[...])
    for n, (i, j, k) in enumerate(everyone):
        own_gain = jnp.concatenate(
            [gains[at % 128:at % 128 + 16, at // 128:at // 128 + 1] for at in range(n * cols, (n + 1) * cols, 16)], axis=0)
        normed[n * cols:(n + 1) * cols, :] = (a_all[i, j, k].astype(f32) * inverse * own_gain).astype(bf)

    def product(i, total):
        at = pl.multiple_of(i * 512, 512)
        return total + jnp.dot(
            w_all[:, pl.ds(at, 512)], normed[pl.ds(at, 512), :], preferred_element_type=f32)

    both = lax.fori_loop(0, width // 512, product, jnp.zeros((4 * pad, 128), f32))
    gate, up = both[:2 * pad], both[2 * pad:]
    hidden = (gate / (1.0 + jnp.exp(-gate)) * up).astype(bf)
    hidden = jnp.concatenate([hidden, jnp.zeros((128 - 2 * pad, 128), bf)], axis=0)

    def piece(core, xx, zz):
        at = pl.multiple_of(dp_of(zz, xx, core) * cols, 16)
        return jnp.dot(d_cols[pl.ds(at, cols), :], hidden, preferred_element_type=f32)

    c_copies = []
    for zz in far_first:
        for k in range(NX):
            down[k, zz] = piece(1 - c, k, zz).astype(bf)
        c_copies.append(remote(down.at[:, zz], dc_buf.at[:, zz], twin))
    x_copies = []
    for zz, c_copy in zip(far_first, c_copies):
        c_copy.wait()
        sent = []
        for k, peer in enumerate(x_peers):
            d_mine[peer, zz] = (piece(c, peer, zz) + dc_buf[peer, zz].astype(f32)).astype(bf)
            sent.append(remote(d_mine.at[peer, zz], dx_buf.at[k, zz], (dp_of(z, peer, c), tp)))
        x_copies.append(sent)
    copies = []
    for zi, zz, sent in zip(far_index, far_first, x_copies):
        final = piece(c, x, zz) + dc_buf[x, zz].astype(f32)
        finish(sent)
        final = final + sum(dx_buf[k, zz].astype(f32) for k in range(3))
        if zi > 0:
            dz_src[zi - 1] = final.astype(bf)
            copies.append(remote(dz_src.at[zi - 1], dz_buf.at[zi - 1], (dp_of(zz, x, c), tp)))
    finish(copies)
    for k in range(7):
        final = final + dz_buf[k].astype(f32)
    share = cols // 4
    empty = jnp.zeros((y_out.shape[1] - share, 128), f32)
    for k in range(4):
        y_out[k] = jnp.concatenate([final[k * share:(k + 1) * share], empty], axis=0)
    y_in[tp] = y_out[tp]
    finish([remote(y_out.at[peer], y_in.at[tp], (me, peer)) for peer in y_peers])
    for t in range(2):
        own = attended[t].astype(f32)
        base = own[:share]
        for k in range(1, 4):
            base = jnp.where(tp == k, own[k * share:(k + 1) * share], base)
        lay_ref[t] = (base + (y_in[t] + y_in[t + 2])[:share]).astype(bf)


def tail(h, st, wo, res, gain, g0, g1, u0, u1, d0, d1, collective_id):
    vmem = pl.BlockSpec(memory_space=pltpu.VMEM)
    h = h.reshape((NC, NX, NZ) + h.shape[1:])
    rows, vd = h.shape[3:]
    cols, width = wo.shape[0], g0.shape[1]
    bf, f32 = jnp.bfloat16, jnp.float32
    pad = -(-g0.shape[0] // 16) * 16
    share = cols // 4
    tall = -(-share // 8) * 8
    shapes = [
        ((NX, NZ, rows, vd), bf), ((2, 32, 128), f32), ((NX, NZ, rows, vd), bf), ((2, 32, 128), f32),
        ((3, NZ, rows, vd), bf), ((3, 2, NZ, 128), f32), ((NZ, rows, vd), bf), ((NZ, 8, 128), f32),
        ((7, rows, vd), bf), ((7, 8, 128), f32),
        ((NZ, NX, NC, rows, vd), bf), ((NDP * rows, vd), f32), ((4,) + res.shape, bf),
        ((NZ, NX, NC, cols, 128), bf), ((width, 128), bf), ((4 * pad, width), bf), ((width, 128), bf),
        ((NX, NZ, cols, 128), bf), ((NX, NZ, cols, 128), bf), ((NX, NZ, cols, 128), bf), ((3, NZ, cols, 128), bf),
        ((7, cols, 128), bf), ((7, cols, 128), bf), ((4, tall, 128), f32), ((4, tall, 128), f32),
    ]
    return pl.pallas_call(
        tail_kernel,
        out_shape=(
            jax.ShapeDtypeStruct(res.shape, bf),
            jax.ShapeDtypeStruct((2, share, 128), bf),
        ),
        in_specs=[vmem] * 11,
        out_specs=(vmem, vmem),
        scratch_shapes=[pltpu.VMEM(shape, kind) for shape, kind in shapes]
        + [pltpu.SemaphoreType.DMA((168,)), pltpu.SemaphoreType.DMA((168,))],
        compiler_params=pltpu.CompilerParams(
            collective_id=collective_id, has_side_effects=True, vmem_limit_bytes=40 * 1024 * 1024),
        name="tail",
    )(h, st, wo, res, gain, g0, g1, u0, u1, d0, d1)


def per_device(
    pool, pool_owner, pool_slot, req_len, query, new_kv, resid, w_uv, w_out, ffn_gain, w_gate, w_up, w_down,
):
    bf = jnp.bfloat16
    steps, requests, heads, key = query.shape
    width = pool.shape[1]
    swap = [(0, 1), (1, 0), (2, 3), (3, 2)]
    gate_t, up_t = w_gate.T, w_up.T
    gate_o, up_o, down_o = (lax.ppermute(w, "tp", swap) for w in (gate_t, up_t, w_down))

    info = jnp.stack([req_len // width, req_len % width], axis=1).reshape(4).astype(bf)
    info = jnp.broadcast_to(jnp.pad(info, (0, 60))[None], (4 * heads, 64))
    rows = jnp.transpose(query, (1, 0, 2, 3)).reshape(4 * heads, key)
    gain = ffn_gain.reshape(-1, 128)
    q_all = gather_dp(jnp.concatenate([rows, info], axis=1), 1)
    head_part, stats = attend(pool_owner, pool_slot, q_all, jnp.swapaxes(pool, 1, 2), new_kv, w_uv)

    attended, layer = tail(
        head_part, stats, w_out.T, jnp.swapaxes(resid, 1, 2), gain, gate_t, gate_o, up_t, up_o, w_down, down_o, 2
    )
    return jnp.swapaxes(attended, 1, 2), jnp.swapaxes(layer, 1, 2)


def solution(mesh):
    in_specs = (
        P("dp", None, None),
        P("dp"),
        P("dp"),
        P("dp"),
        P(None, "dp", "tp", None),
        P(None, "dp", None),
        P(None, None, "dp"),
        P("tp", None, None),
        P("tp", "dp"),
        P(),
        P(None, ("dp", "tp")),
        P(None, ("dp", "tp")),
        P(("dp", "tp"), None),
    )
    out_specs = (P(None, None, "dp"), P(None, None, ("dp", "tp")))
    return jax.shard_map(
        per_device, mesh=mesh, in_specs=in_specs, out_specs=out_specs, check_vma=False
    )
```
